32 devices in a mesh: grid: 16 (over z, y, x), mode: 2 (over core).
Axes of the slice: x: 2, y: 2, z: 4, core: 2. Of those that a mesh axis runs over, the one named last changes fastest.
Arguments:
- modes: bfloat16 [8, 3, 32, 32, 128], P('mode', None, 'grid'), may hold values from -0.29882812 to 0.29882812
- eigenvalues: float32 [8], P('mode'), may hold values from 2 to 50
- density: float32 [32, 32, 128], P('grid'), may hold values from 0.1 to 1
Outputs:
- gradient: float32 [32, 32, 128], P('grid')
The draws below stay inside these ranges and needn't reach their ends.
All inputs are finite; a program needn't handle non-finite values.
Results may differ from the reference program's by a relative error of at most 0.006.
Values may be sent and summed in bfloat16 or wider, within the bound.
A program may use at most 64 MiB of HBM per device.

```python
import math
import jax
import jax.numpy as jnp
import numpy as np
from jax import lax

EX = 128
EY = 32
MODES = 8
NZ = 32


def block_levels(stream_key, shape, cuts, low, high):
    gain, own = 1.0, jax.random.fold_in(stream_key, 6)
    for axis_at, shards_of in cuts:
        steps = jnp.exp(jax.random.uniform(jax.random.fold_in(own, axis_at), (shards_of,), jnp.float32, low / len(cuts), high / len(cuts)))
        gain = gain * jnp.repeat(steps, shape[axis_at] // shards_of).reshape([-1 if axis == axis_at else 1 for axis in range(len(shape))])
    return gain


def noise(stream_key, dims, scale, most, shards=(), kind=jnp.bfloat16):
    level = block_levels(stream_key, dims, shards, -0.22, 0.18) if shards else 1.0
    entries = jax.random.normal(stream_key, dims, jnp.float32) * scale * level
    return jnp.minimum(jnp.maximum(entries, -most), most).astype(kind)


def setup_inputs(seed: int = 0) -> dict:
    keys = jax.random.split(jax.random.key(seed), 4)
    modes = noise(keys[0], (MODES, 3, NZ, EY, EX), 0.05, 0.29882812, ((0, 2), (2, 16)))
    eigenvalues = jnp.clip(jnp.exp(math.log(50.0) - 3.218876 * jax.random.uniform(keys[1], (MODES,), jnp.float32) ** block_levels(keys[1], (MODES,), ((0, 2),), -0.2, 0.2)), 2.0, 50.0)
    density = jnp.clip(0.1 + 0.9 * jax.random.uniform(keys[2], (NZ, EY, EX), jnp.float32) ** block_levels(keys[2], (NZ, EY, EX), ((0, 16),), -0.2, 0.2), 0.1, 1.0)
    return {"modes": modes, "eigenvalues": eigenvalues, "density": density}


def element_tables():
    poisson = 0.3
    lame_first = poisson / ((1.0 + poisson) * (1.0 - 2.0 * poisson))
    shear = 0.5 / (1.0 + poisson)
    elastic = np.zeros((6, 6))
    elastic[:3, :3] = lame_first
    for axis_bit in range(3):
        elastic[axis_bit, axis_bit] += 2.0 * shear
        elastic[axis_bit + 3, axis_bit + 3] = shear
    stiffness = np.zeros((24, 24))
    mass_small = np.zeros((8, 8))
    point = 1.0 / np.sqrt(3.0)
    for gauss in range(8):
        coords = [point * (2 * (gauss >> axis_bit & 1) - 1) for axis_bit in range(3)]
        shape_values = np.zeros(8)
        grads = np.zeros((3, 8))
        for corner in range(8):
            signs = [2 * (corner >> axis_bit & 1) - 1 for axis_bit in range(3)]
            factors = [1.0 + signs[axis_bit] * coords[axis_bit] for axis_bit in range(3)]
            shape_values[corner] = 0.125 * factors[0] * factors[1] * factors[2]
            grads[0, corner] = 0.25 * signs[0] * factors[1] * factors[2]
            grads[1, corner] = 0.25 * signs[1] * factors[0] * factors[2]
            grads[2, corner] = 0.25 * signs[2] * factors[0] * factors[1]
        strain = np.zeros((6, 24))
        for corner in range(8):
            column = 3 * corner
            strain[0, column] = grads[0, corner]
            strain[1, column + 1] = grads[1, corner]
            strain[2, column + 2] = grads[2, corner]
            strain[3, column] = grads[1, corner]
            strain[3, column + 1] = grads[0, corner]
            strain[4, column + 1] = grads[2, corner]
            strain[4, column + 2] = grads[1, corner]
            strain[5, column] = grads[2, corner]
            strain[5, column + 2] = grads[0, corner]
        stiffness = stiffness + strain.T @ elastic @ strain * 0.125
        mass_small = mass_small + np.outer(shape_values, shape_values) * 0.125
    mass = np.kron(mass_small, np.eye(3))
    return np.concatenate([stiffness, mass], 0).astype(np.float32)

def element_forms(field, table):
    depth = field.shape[1] - 1
    height = field.shape[2]
    width = field.shape[3]
    padded = jnp.pad(field, ((0, 0), (0, 0), (0, 1), (0, 1)))
    pieces = []
    for corner in range(8):
        x_off = corner & 1
        y_off = corner >> 1 & 1
        z_off = corner >> 2
        for component in range(3):
            pieces.append(padded[component, z_off:z_off + depth, y_off:y_off + height, x_off:x_off + width].reshape(-1))
    stacked = jnp.stack(pieces)
    images = jnp.dot(table, stacked, preferred_element_type=jnp.float32)
    values = stacked.astype(jnp.float32)
    stiff_form = lax.optimization_barrier(jnp.sum(values * images[:24], 0)).reshape(depth, height, width)
    mass_form = lax.optimization_barrier(jnp.sum(values * images[24:], 0)).reshape(depth, height, width)
    return (stiff_form, mass_form)

def filter_weights():
    listed = []
    for z_step in range(-2, 3):
        for y_step in range(-2, 3):
            for x_step in range(-2, 3):
                weight = 2.5 - float(np.sqrt(z_step * z_step + y_step * y_step + x_step * x_step))
                if weight > 0.0:
                    listed.append((z_step, y_step, x_step, weight))
    return listed

def apply_stencil(padded, weights):
    depth = padded.shape[0] - 4
    height = padded.shape[1] - 4
    width = padded.shape[2] - 4
    total = jnp.zeros((depth, height, width), padded.dtype)
    for z_step, y_step, x_step, weight in weights:
        total = total + weight * padded[2 + z_step:2 + z_step + depth, 2 + y_step:2 + y_step + height, 2 + x_step:2 + x_step + width]
    return total

def reference(modes, eigenvalues, density):
    table = jnp.asarray(element_tables()).astype(jnp.bfloat16)

    def one_mode(carry, inputs):
        field, value = inputs
        field = jnp.pad(field, ((0, 0), (0, 1), (0, 0), (0, 0)))
        stiff_form, mass_form = element_forms(field, table)
        return ((carry[0] + stiff_form, carry[1] + value * mass_form), None)
    zeros = jnp.zeros(density.shape, jnp.float32)
    (stiff_total, mass_total), unused = lax.scan(one_mode, (zeros, zeros), (modes, eigenvalues))
    slope = 3.0 * (1.0 - 0.001) * density * density
    sensitivity = slope * stiff_total - mass_total
    weights = filter_weights()
    totals = apply_stencil(jnp.pad(jnp.ones(density.shape, jnp.float32), 2), weights)
    scaled = sensitivity / totals
    return apply_stencil(jnp.pad(scaled, 2), weights)
```

```python
import functools

import jax
import jax.numpy as jnp
import ml_dtypes
import numpy as np
from jax import lax
from jax.experimental import pallas as pl
from jax.experimental.pallas import tpu as pltpu
from jax.sharding import PartitionSpec as P

MESH = pl.DeviceIdType.MESH


def element_tables():
    poisson = 0.3
    lame_first = poisson / ((1.0 + poisson) * (1.0 - 2.0 * poisson))
    shear = 0.5 / (1.0 + poisson)
    elastic = np.zeros((6, 6))
    elastic[:3, :3] = lame_first
    for axis_bit in range(3):
        elastic[axis_bit, axis_bit] += 2.0 * shear
        elastic[axis_bit + 3, axis_bit + 3] = shear
    stiffness = np.zeros((24, 24))
    mass_small = np.zeros((8, 8))
    point = 1.0 / np.sqrt(3.0)
    for gauss in range(8):
        coords = [point * (2 * (gauss >> axis_bit & 1) - 1) for axis_bit in range(3)]
        shape_values = np.zeros(8)
        grads = np.zeros((3, 8))
        for corner in range(8):
            signs = [2 * (corner >> axis_bit & 1) - 1 for axis_bit in range(3)]
            factors = [1.0 + signs[axis_bit] * coords[axis_bit] for axis_bit in range(3)]
            shape_values[corner] = 0.125 * factors[0] * factors[1] * factors[2]
            grads[0, corner] = 0.25 * signs[0] * factors[1] * factors[2]
            grads[1, corner] = 0.25 * signs[1] * factors[0] * factors[2]
            grads[2, corner] = 0.25 * signs[2] * factors[0] * factors[1]
        strain = np.zeros((6, 24))
        for corner in range(8):
            column = 3 * corner
            strain[0, column] = grads[0, corner]
            strain[1, column + 1] = grads[1, corner]
            strain[2, column + 2] = grads[2, corner]
            strain[3, column] = grads[1, corner]
            strain[3, column + 1] = grads[0, corner]
            strain[4, column + 1] = grads[2, corner]
            strain[4, column + 2] = grads[1, corner]
            strain[5, column] = grads[2, corner]
            strain[5, column + 2] = grads[0, corner]
        stiffness = stiffness + strain.T @ elastic @ strain * 0.125
        mass_small = mass_small + np.outer(shape_values, shape_values) * 0.125
    mass = np.kron(mass_small, np.eye(3))
    return np.concatenate([stiffness, mass], 0).astype(np.float32)


def transformed_terms():
    table = element_tables().astype(ml_dtypes.bfloat16).astype(np.float64)
    change = np.ones((8, 8))
    for corner in range(8):
        for pattern in range(8):
            for bit in range(3):
                if pattern >> bit & 1 and not corner >> bit & 1:
                    change[corner, pattern] *= -1.0
    stiff, mass = (
        np.einsum("is,icjd,jt->sctd", change, part.reshape(8, 3, 8, 3), change).reshape(24, 24) / 64.0
        for part in (table[:24], table[24:])
    )
    assert np.abs(mass - np.diag(np.diag(mass))).max() < 1e-12
    squares, crosses = {}, {}
    for row in range(24):
        key = (round(stiff[row, row], 12), round(mass[row, row], 12))
        squares.setdefault(key, []).append(row)
        for column in range(row):
            value = round(stiff[row, column] + stiff[column, row], 12)
            if value != 0.0:
                crosses.setdefault(value, []).append((row, column))
    return squares, crosses


def next_in(value, axis):
    size = value.shape[axis]
    place = lax.broadcasted_iota(jnp.int32, value.shape, axis)
    return jnp.where(place == size - 1, 0.0, pltpu.roll(value, size - 1, axis))


def both_sides(value, steps, axis):
    size = value.shape[axis]
    place = lax.broadcasted_iota(jnp.int32, value.shape, axis)
    ahead = jnp.where(place >= size - steps, 0.0, pltpu.roll(value, size - steps, axis))
    behind = jnp.where(place < steps, 0.0, pltpu.roll(value, steps, axis))
    return ahead + behind


def plane_terms(plane):
    value = plane.astype(jnp.float32)
    ahead = next_in(value, 1)
    along_x = (value + ahead, ahead - value)
    shifted = [next_in(part, 0) for part in along_x]
    return [along_x[0] + shifted[0], along_x[1] + shifted[1], shifted[0] - along_x[0], shifted[1] - along_x[1]]


def add_all(values):
    values = list(values)
    while len(values) > 1:
        values = [sum(values[i : i + 2][1:], values[i]) for i in range(0, len(values), 2)]
    return values[0]


def element_form(low, high):
    squares, crosses = transformed_terms()
    wave = {}
    for component in range(3):
        for pattern in range(4):
            wave[3 * pattern + component] = low[component][pattern] + high[component][pattern]
            wave[3 * (pattern + 4) + component] = high[component][pattern] - low[component][pattern]
    stiff, by_mass = [], {}
    for (stiff_value, mass_value), rows in squares.items():
        total = add_all(wave[row] * wave[row] for row in rows)
        if stiff_value != 0.0:
            stiff.append(stiff_value * total)
        by_mass.setdefault(mass_value, []).append(total)
    for value, pairs in crosses.items():
        stiff.append(value * add_all(wave[row] * wave[column] for row, column in pairs))
    mass = [value * add_all(totals) for value, totals in by_mass.items()]
    return add_all(stiff), add_all(mass)


def filtered(near, one, two):
    def weight(square):
        return max(0.0, 2.5 - float(np.sqrt(square)))

    rings = {
        0: near,
        1: both_sides(near, 1, 0) + one,
        2: both_sides(one, 1, 0),
        4: both_sides(near, 2, 0) + two,
        5: both_sides(one, 2, 0) + both_sides(two, 1, 0),
    }

    def column(steps):
        return add_all(
            weight(square + steps * steps) * ring
            for square, ring in rings.items()
            if weight(square + steps * steps) > 0.0
        )

    return column(0) + both_sides(column(1), 1, 1) + both_sides(column(2), 2, 1)


def kernel(
    layers, groups, modes_ref, eigen_ref, density_ref, out_ref,
    field, upper, terms, dens, share,
    field_sem, dens_sem, plane_send, plane_recv, share_send, share_recv,
):
    grid, mode = lax.axis_index("grid"), lax.axis_index("mode")
    count, depth = modes_ref.shape[0], modes_ref.shape[2]
    height, width = modes_ref.shape[3:]
    last = layers - 1

    def load(index):
        return pltpu.make_async_copy(modes_ref.at[index], field.at[index], field_sem.at[index])

    for index in range(count):
        load(index).start()
    density_copy = pltpu.make_async_copy(density_ref, dens, dens_sem)
    density_copy.start()

    partners = [(step, turn) for step in (-1, 1, 0) for turn in range(groups) if (step, turn) != (0, 0)]

    def target(step, turn):
        return (grid + step, lax.rem(mode + turn, groups))

    def there(step, body):
        if step < 0:
            pl.when(grid > 0)(body)
        elif step > 0:
            pl.when(grid < last)(body)
        else:
            body()

    barrier = pltpu.get_barrier_semaphore()
    for step, turn in partners:
        there(step, lambda: pl.semaphore_signal(barrier, inc=1, device_id=target(step, turn), device_id_type=MESH))
    sides = jnp.minimum(grid, 1) + jnp.minimum(last - grid, 1)
    pl.semaphore_wait(barrier, groups - 1 + groups * sides)

    def plane_copy(index):
        return pltpu.make_async_remote_copy(
            src_ref=modes_ref.at[index, :, 0],
            dst_ref=upper.at[index],
            send_sem=plane_send.at[index],
            recv_sem=plane_recv.at[index],
            device_id=(jnp.maximum(grid - 1, 0), mode),
            device_id_type=MESH,
        )

    @pl.when(grid > 0)
    def _():
        for index in range(count):
            plane_copy(index).start()

    @pl.when(grid == last)
    def _():
        upper[...] = jnp.zeros_like(upper)
        share[2] = jnp.zeros_like(share[2])

    @pl.when(grid == 0)
    def _():
        share[0] = jnp.zeros_like(share[0])

    ones = jnp.ones((height, width), jnp.float32)
    totals = []
    for layer in range(depth):
        place = grid * depth + layer

        def inside(steps):
            low = jnp.minimum(jnp.maximum(place - steps + 1, 0), 1)
            high = jnp.minimum(jnp.maximum(layers * depth - place - steps, 0), 1)
            return (low + high).astype(jnp.float32) * ones

        totals.append(filtered(ones, inside(1), inside(2)))

    zeros = jnp.zeros((height, width), jnp.float32)

    def first(index, carry):
        load(index).wait()
        low = [plane_terms(field[index, component, 0]) for component in range(3)]
        high = [plane_terms(field[index, component, 1]) for component in range(3)]
        for component in range(3):
            for pattern in range(4):
                terms[index, component, pattern] = high[component][pattern]
        stiff, mass = element_form(low, high)
        return carry[0] + stiff, carry[1] + eigen_ref[index] * mass

    def second(index, carry):
        @pl.when(grid < last)
        def _():
            plane_copy(index).wait_recv()

        low = [[terms[index, component, pattern] for pattern in range(4)] for component in range(3)]
        high = [plane_terms(upper[index, component]) for component in range(3)]
        stiff, mass = element_form(low, high)
        return carry[0] + stiff, carry[1] + eigen_ref[index] * mass

    def share_copy(layer, step, turn):
        return pltpu.make_async_remote_copy(
            src_ref=share.at[1, mode, layer],
            dst_ref=share.at[1 - step, mode, layer],
            send_sem=share_send.at[layer, step + 1, turn],
            recv_sem=share_recv.at[layer, 1 - step, mode],
            device_id=target(step, turn),
            device_id_type=MESH,
        )

    def arrived(layer, step, turn):
        source = lax.rem(mode + turn, groups)
        return pltpu.make_async_remote_copy(
            src_ref=share.at[1, mode, layer],
            dst_ref=share.at[1 + step, source, layer],
            send_sem=share_send.at[layer, step + 1, turn],
            recv_sem=share_recv.at[layer, 1 + step, source],
            device_id=target(step, turn),
            device_id_type=MESH,
        )

    def finish(layer, stiff, mass):
        slope = 3.0 * (1.0 - 0.001) * dens[layer] * dens[layer]
        share[1, mode, layer] = ((slope * stiff - mass) / totals[layer]).astype(jnp.bfloat16)
        for step, turn in partners:
            there(step, lambda: share_copy(layer, step, turn).start())

    stiff, mass = lax.fori_loop(0, count, first, (zeros, zeros))
    density_copy.wait()
    finish(0, stiff, mass)
    stiff, mass = lax.fori_loop(0, count, second, (zeros, zeros))
    finish(1, stiff, mass)

    for layer in range(depth):
        for step, turn in partners:
            there(step, lambda: arrived(layer, step, turn).wait_recv())

    def whole(place, layer):
        return add_all(share[place, group, layer].astype(jnp.float32) for group in range(groups))

    stack = [whole(place, layer) for place in range(3) for layer in range(depth)]
    for layer in range(depth):
        at = depth + layer
        out_ref[layer] = filtered(stack[at], stack[at - 1] + stack[at + 1], stack[at - 2] + stack[at + 2])

    for layer in range(depth):
        for step, turn in partners:
            there(step, lambda: share_copy(layer, step, turn).wait_send())

    @pl.when(grid > 0)
    def _():
        for index in range(count):
            plane_copy(index).wait_send()


def local(layers, groups, modes, eigenvalues, density):
    count, _, depth, height, width = modes.shape
    assert depth == 2
    return pl.pallas_call(
        functools.partial(kernel, layers, groups),
        out_shape=jax.ShapeDtypeStruct(density.shape, jnp.float32),
        in_specs=[
            pl.BlockSpec(memory_space=pl.ANY),
            pl.BlockSpec(memory_space=pltpu.SMEM),
            pl.BlockSpec(memory_space=pl.ANY),
        ],
        out_specs=pl.BlockSpec(memory_space=pltpu.VMEM),
        scratch_shapes=[
            pltpu.VMEM(modes.shape, jnp.bfloat16),
            pltpu.VMEM((count, 3, height, width), jnp.bfloat16),
            pltpu.VMEM((count, 3, 4, height, width), jnp.float32),
            pltpu.VMEM(density.shape, jnp.float32),
            pltpu.VMEM((3, groups, depth, height, width), jnp.bfloat16),
            pltpu.SemaphoreType.DMA((count,)),
            pltpu.SemaphoreType.DMA,
            pltpu.SemaphoreType.DMA((count,)),
            pltpu.SemaphoreType.DMA((count,)),
            pltpu.SemaphoreType.DMA((depth, 3, groups)),
            pltpu.SemaphoreType.DMA((depth, 3, groups)),
        ],
        compiler_params=pltpu.CompilerParams(
            collective_id=0, has_side_effects=True, vmem_limit_bytes=24 * 1024 * 1024
        ),
        name="sensitivities",
    )(modes, eigenvalues, density)


def solution(mesh):
    in_specs = (P("mode", None, "grid", None, None), P("mode"), P("grid", None, None))
    body = functools.partial(local, mesh.shape["grid"], mesh.shape["mode"])
    return jax.shard_map(body, mesh=mesh, in_specs=in_specs, out_specs=P("grid", None, None), check_vma=False)
```

```python
import functools

import jax
import jax.numpy as jnp
import ml_dtypes
import numpy as np
from jax import lax
from jax.experimental import pallas as pl
from jax.experimental.pallas import tpu as pltpu
from jax.sharding import PartitionSpec as P

MESH = pl.DeviceIdType.MESH


def element_tables():
    poisson = 0.3
    lame_first = poisson / ((1.0 + poisson) * (1.0 - 2.0 * poisson))
    shear = 0.5 / (1.0 + poisson)
    elastic = np.zeros((6, 6))
    elastic[:3, :3] = lame_first
    for axis_bit in range(3):
        elastic[axis_bit, axis_bit] += 2.0 * shear
        elastic[axis_bit + 3, axis_bit + 3] = shear
    stiffness = np.zeros((24, 24))
    mass_small = np.zeros((8, 8))
    point = 1.0 / np.sqrt(3.0)
    for gauss in range(8):
        coords = [point * (2 * (gauss >> axis_bit & 1) - 1) for axis_bit in range(3)]
        shape_values = np.zeros(8)
        grads = np.zeros((3, 8))
        for corner in range(8):
            signs = [2 * (corner >> axis_bit & 1) - 1 for axis_bit in range(3)]
            factors = [1.0 + signs[axis_bit] * coords[axis_bit] for axis_bit in range(3)]
            shape_values[corner] = 0.125 * factors[0] * factors[1] * factors[2]
            grads[0, corner] = 0.25 * signs[0] * factors[1] * factors[2]
            grads[1, corner] = 0.25 * signs[1] * factors[0] * factors[2]
            grads[2, corner] = 0.25 * signs[2] * factors[0] * factors[1]
        strain = np.zeros((6, 24))
        for corner in range(8):
            column = 3 * corner
            strain[0, column] = grads[0, corner]
            strain[1, column + 1] = grads[1, corner]
            strain[2, column + 2] = grads[2, corner]
            strain[3, column] = grads[1, corner]
            strain[3, column + 1] = grads[0, corner]
            strain[4, column + 1] = grads[2, corner]
            strain[4, column + 2] = grads[1, corner]
            strain[5, column] = grads[2, corner]
            strain[5, column + 2] = grads[0, corner]
        stiffness = stiffness + strain.T @ elastic @ strain * 0.125
        mass_small = mass_small + np.outer(shape_values, shape_values) * 0.125
    mass = np.kron(mass_small, np.eye(3))
    return np.concatenate([stiffness, mass], 0).astype(np.float32)


def transformed_terms():
    table = element_tables().astype(ml_dtypes.bfloat16).astype(np.float64)
    change = np.ones((8, 8))
    for corner in range(8):
        for pattern in range(8):
            for bit in range(3):
                if pattern >> bit & 1 and not corner >> bit & 1:
                    change[corner, pattern] *= -1.0
    stiff, mass = (
        np.einsum("is,icjd,jt->sctd", change, part.reshape(8, 3, 8, 3), change).reshape(24, 24) / 64.0
        for part in (table[:24], table[24:])
    )
    assert np.abs(mass - np.diag(np.diag(mass))).max() < 1e-12
    squares, crosses = {}, {}
    for row in range(24):
        key = (round(stiff[row, row], 12), round(mass[row, row], 12))
        squares.setdefault(key, []).append(row)
        for column in range(row):
            value = round(stiff[row, column] + stiff[column, row], 12)
            if value != 0.0:
                crosses.setdefault(value, []).append((row, column))
    return squares, crosses


def next_in(value, axis):
    size = value.shape[axis]
    place = lax.broadcasted_iota(jnp.int32, value.shape, axis)
    return jnp.where(place == size - 1, 0.0, pltpu.roll(value, size - 1, axis))


def both_sides(value, steps, axis):
    size = value.shape[axis]
    place = lax.broadcasted_iota(jnp.int32, value.shape, axis)
    ahead = jnp.where(place >= size - steps, 0.0, pltpu.roll(value, size - steps, axis))
    behind = jnp.where(place < steps, 0.0, pltpu.roll(value, steps, axis))
    return ahead + behind


def plane_terms(plane):
    value = plane.astype(jnp.float32)
    ahead = next_in(value, 1)
    along_x = (value + ahead, ahead - value)
    shifted = [next_in(part, 0) for part in along_x]
    return [along_x[0] + shifted[0], along_x[1] + shifted[1], shifted[0] - along_x[0], shifted[1] - along_x[1]]


def add_all(values):
    values = list(values)
    while len(values) > 1:
        values = [sum(values[i : i + 2][1:], values[i]) for i in range(0, len(values), 2)]
    return values[0]


def element_form(low, high):
    squares, crosses = transformed_terms()
    wave = {}
    for component in range(3):
        for pattern in range(4):
            wave[3 * pattern + component] = low[component][pattern] + high[component][pattern]
            wave[3 * (pattern + 4) + component] = high[component][pattern] - low[component][pattern]
    stiff, by_mass = [], {}
    for (stiff_value, mass_value), rows in squares.items():
        total = add_all(wave[row] * wave[row] for row in rows)
        if stiff_value != 0.0:
            stiff.append(stiff_value * total)
        by_mass.setdefault(mass_value, []).append(total)
    for value, pairs in crosses.items():
        stiff.append(value * add_all(wave[row] * wave[column] for row, column in pairs))
    mass = [value * add_all(totals) for value, totals in by_mass.items()]
    return add_all(stiff), add_all(mass)


def filtered(near, one, two):
    def weight(square):
        return max(0.0, 2.5 - float(np.sqrt(square)))

    rings = {
        0: near,
        1: both_sides(near, 1, 0) + one,
        2: both_sides(one, 1, 0),
        4: both_sides(near, 2, 0) + two,
        5: both_sides(one, 2, 0) + both_sides(two, 1, 0),
    }

    def column(steps):
        return add_all(
            weight(square + steps * steps) * ring
            for square, ring in rings.items()
            if weight(square + steps * steps) > 0.0
        )

    return column(0) + both_sides(column(1), 1, 1) + both_sides(column(2), 2, 1)


def kernel(
    layers, groups, modes_ref, eigenvalues_ref, density_ref, out_ref,
    eigen_ref, field, upper, terms, dens, share,
    eigen_sem, field_sem, dens_sem, plane_send, plane_recv, share_send, share_recv,
):
    grid, mode = lax.axis_index("grid"), lax.axis_index("mode")
    count, depth = modes_ref.shape[0], modes_ref.shape[2]
    height, width = modes_ref.shape[3:]
    last = layers - 1

    partners = [(step, turn) for step in (-1, 1, 0) for turn in range(groups) if (step, turn) != (0, 0)]

    def target(step, turn):
        return (grid + step, lax.rem(mode + turn, groups))

    def there(step, body):
        if step < 0:
            pl.when(grid > 0)(body)
        elif step > 0:
            pl.when(grid < last)(body)
        else:
            body()

    barrier = pltpu.get_barrier_semaphore()
    for step, turn in partners:
        there(step, lambda: pl.semaphore_signal(barrier, inc=1, device_id=target(step, turn), device_id_type=MESH))

    def load(index):
        return pltpu.make_async_copy(modes_ref.at[index], field.at[index], field_sem.at[index])

    eigen_copy = pltpu.make_async_copy(eigenvalues_ref, eigen_ref, eigen_sem)
    eigen_copy.start()
    for index in range(count):
        load(index).start()
    density_copy = pltpu.make_async_copy(density_ref, dens, dens_sem)
    density_copy.start()

    sides = jnp.minimum(grid, 1) + jnp.minimum(last - grid, 1)
    pl.semaphore_wait(barrier, groups - 1 + groups * sides)

    def plane_copy(index):
        return pltpu.make_async_remote_copy(
            src_ref=modes_ref.at[index, :, 0],
            dst_ref=upper.at[index],
            send_sem=plane_send.at[index],
            recv_sem=plane_recv.at[index],
            device_id=(jnp.maximum(grid - 1, 0), mode),
            device_id_type=MESH,
        )

    @pl.when(grid > 0)
    def _():
        for index in range(count):
            plane_copy(index).start()

    @pl.when(grid == last)
    def _():
        upper[...] = jnp.zeros_like(upper)
        share[2] = jnp.zeros_like(share[2])

    @pl.when(grid == 0)
    def _():
        share[0] = jnp.zeros_like(share[0])

    ones = jnp.ones((height, width), jnp.float32)
    totals = []
    for layer in range(depth):
        place = grid * depth + layer

        def inside(steps):
            low = jnp.minimum(jnp.maximum(place - steps + 1, 0), 1)
            high = jnp.minimum(jnp.maximum(layers * depth - place - steps, 0), 1)
            return (low + high).astype(jnp.float32) * ones

        totals.append(filtered(ones, inside(1), inside(2)))

    zeros = jnp.zeros((height, width), jnp.float32)

    def first(index, carry):
        load(index).wait()
        low = [plane_terms(field[index, component, 0]) for component in range(3)]
        high = [plane_terms(field[index, component, 1]) for component in range(3)]
        for component in range(3):
            for pattern in range(4):
                terms[index, component, pattern] = high[component][pattern]
        stiff, mass = element_form(low, high)
        return carry[0] + stiff, carry[1] + eigen_ref[index] * mass

    def second(index, carry):
        @pl.when(grid < last)
        def _():
            plane_copy(index).wait_recv()

        low = [[terms[index, component, pattern] for pattern in range(4)] for component in range(3)]
        high = [plane_terms(upper[index, component]) for component in range(3)]
        stiff, mass = element_form(low, high)
        return carry[0] + stiff, carry[1] + eigen_ref[index] * mass

    def share_copy(layer, step, turn):
        return pltpu.make_async_remote_copy(
            src_ref=share.at[1, mode, layer],
            dst_ref=share.at[1 - step, mode, layer],
            send_sem=share_send.at[layer, step + 1, turn],
            recv_sem=share_recv.at[layer, 1 - step, mode],
            device_id=target(step, turn),
            device_id_type=MESH,
        )

    def arrived(layer, step, turn):
        source = lax.rem(mode + turn, groups)
        return pltpu.make_async_remote_copy(
            src_ref=share.at[1, mode, layer],
            dst_ref=share.at[1 + step, source, layer],
            send_sem=share_send.at[layer, step + 1, turn],
            recv_sem=share_recv.at[layer, 1 + step, source],
            device_id=target(step, turn),
            device_id_type=MESH,
        )

    def finish(layer, stiff, mass):
        slope = 3.0 * (1.0 - 0.001) * dens[layer] * dens[layer]
        share[1, mode, layer] = ((slope * stiff - mass) / totals[layer]).astype(jnp.bfloat16)
        for step, turn in partners:
            there(step, lambda: share_copy(layer, step, turn).start())

    eigen_copy.wait()
    stiff, mass = lax.fori_loop(0, count, first, (zeros, zeros))
    density_copy.wait()
    finish(0, stiff, mass)
    stiff, mass = lax.fori_loop(0, count, second, (zeros, zeros))
    finish(1, stiff, mass)

    for layer in range(depth):
        for step, turn in partners:
            there(step, lambda: arrived(layer, step, turn).wait_recv())

    def whole(place, layer):
        return add_all(share[place, group, layer].astype(jnp.float32) for group in range(groups))

    stack = [whole(place, layer) for place in range(3) for layer in range(depth)]
    for layer in range(depth):
        at = depth + layer
        out_ref[layer] = filtered(stack[at], stack[at - 1] + stack[at + 1], stack[at - 2] + stack[at + 2])

    for layer in range(depth):
        for step, turn in partners:
            there(step, lambda: share_copy(layer, step, turn).wait_send())

    @pl.when(grid > 0)
    def _():
        for index in range(count):
            plane_copy(index).wait_send()


def local(layers, groups, modes, eigenvalues, density):
    count, _, depth, height, width = modes.shape
    assert depth == 2
    return pl.pallas_call(
        functools.partial(kernel, layers, groups),
        out_shape=jax.ShapeDtypeStruct(density.shape, jnp.float32),
        in_specs=[
            pl.BlockSpec(memory_space=pltpu.HBM),
            pl.BlockSpec(memory_space=pltpu.HBM),
            pl.BlockSpec(memory_space=pltpu.HBM),
        ],
        out_specs=pl.BlockSpec(memory_space=pltpu.VMEM),
        scratch_shapes=[
            pltpu.SMEM(eigenvalues.shape, jnp.float32),
            pltpu.VMEM(modes.shape, jnp.bfloat16),
            pltpu.VMEM((count, 3, height, width), jnp.bfloat16),
            pltpu.VMEM((count, 3, 4, height, width), jnp.float32),
            pltpu.VMEM(density.shape, jnp.float32),
            pltpu.VMEM((3, groups, depth, height, width), jnp.bfloat16),
            pltpu.SemaphoreType.DMA,
            pltpu.SemaphoreType.DMA((count,)),
            pltpu.SemaphoreType.DMA,
            pltpu.SemaphoreType.DMA((count,)),
            pltpu.SemaphoreType.DMA((count,)),
            pltpu.SemaphoreType.DMA((depth, 3, groups)),
            pltpu.SemaphoreType.DMA((depth, 3, groups)),
        ],
        compiler_params=pltpu.CompilerParams(
            collective_id=0, has_side_effects=True, vmem_limit_bytes=24 * 1024 * 1024
        ),
        name="sensitivities",
    )(modes, eigenvalues, density)


def solution(mesh):
    in_specs = (P("mode", None, "grid", None, None), P("mode"), P("grid", None, None))
    body = functools.partial(local, mesh.shape["grid"], mesh.shape["mode"])
    return jax.shard_map(body, mesh=mesh, in_specs=in_specs, out_specs=P("grid", None, None), check_vma=False)
```

```python
import functools

import jax
import jax.numpy as jnp
import ml_dtypes
import numpy as np
from jax import lax
from jax.experimental import pallas as pl
from jax.experimental.pallas import tpu as pltpu
from jax.sharding import PartitionSpec as P

MESH = pl.DeviceIdType.MESH


def element_tables():
    poisson = 0.3
    lame_first = poisson / ((1.0 + poisson) * (1.0 - 2.0 * poisson))
    shear = 0.5 / (1.0 + poisson)
    elastic = np.zeros((6, 6))
    elastic[:3, :3] = lame_first
    for axis_bit in range(3):
        elastic[axis_bit, axis_bit] += 2.0 * shear
        elastic[axis_bit + 3, axis_bit + 3] = shear
    stiffness = np.zeros((24, 24))
    mass_small = np.zeros((8, 8))
    point = 1.0 / np.sqrt(3.0)
    for gauss in range(8):
        coords = [point * (2 * (gauss >> axis_bit & 1) - 1) for axis_bit in range(3)]
        shape_values = np.zeros(8)
        grads = np.zeros((3, 8))
        for corner in range(8):
            signs = [2 * (corner >> axis_bit & 1) - 1 for axis_bit in range(3)]
            factors = [1.0 + signs[axis_bit] * coords[axis_bit] for axis_bit in range(3)]
            shape_values[corner] = 0.125 * factors[0] * factors[1] * factors[2]
            grads[0, corner] = 0.25 * signs[0] * factors[1] * factors[2]
            grads[1, corner] = 0.25 * signs[1] * factors[0] * factors[2]
            grads[2, corner] = 0.25 * signs[2] * factors[0] * factors[1]
        strain = np.zeros((6, 24))
        for corner in range(8):
            column = 3 * corner
            strain[0, column] = grads[0, corner]
            strain[1, column + 1] = grads[1, corner]
            strain[2, column + 2] = grads[2, corner]
            strain[3, column] = grads[1, corner]
            strain[3, column + 1] = grads[0, corner]
            strain[4, column + 1] = grads[2, corner]
            strain[4, column + 2] = grads[1, corner]
            strain[5, column] = grads[2, corner]
            strain[5, column + 2] = grads[0, corner]
        stiffness = stiffness + strain.T @ elastic @ strain * 0.125
        mass_small = mass_small + np.outer(shape_values, shape_values) * 0.125
    mass = np.kron(mass_small, np.eye(3))
    return np.concatenate([stiffness, mass], 0).astype(np.float32)


def transformed_terms():
    table = element_tables().astype(ml_dtypes.bfloat16).astype(np.float64)
    change = np.ones((8, 8))
    for corner in range(8):
        for pattern in range(8):
            for bit in range(3):
                if pattern >> bit & 1 and not corner >> bit & 1:
                    change[corner, pattern] *= -1.0
    stiff, mass = (
        np.einsum("is,icjd,jt->sctd", change, part.reshape(8, 3, 8, 3), change).reshape(24, 24) / 64.0
        for part in (table[:24], table[24:])
    )
    assert np.abs(mass - np.diag(np.diag(mass))).max() < 1e-12
    squares, crosses = {}, {}
    for row in range(24):
        key = (round(stiff[row, row], 12), round(mass[row, row], 12))
        squares.setdefault(key, []).append(row)
        for column in range(row):
            value = round(stiff[row, column] + stiff[column, row], 12)
            if value != 0.0:
                crosses.setdefault(value, []).append((row, column))
    return squares, crosses


def next_in(value, axis):
    size = value.shape[axis]
    place = lax.broadcasted_iota(jnp.int32, value.shape, axis)
    return jnp.where(place == size - 1, 0.0, pltpu.roll(value, size - 1, axis))


def both_sides(value, steps, axis):
    size = value.shape[axis]
    place = lax.broadcasted_iota(jnp.int32, value.shape, axis)
    ahead = jnp.where(place >= size - steps, 0.0, pltpu.roll(value, size - steps, axis))
    behind = jnp.where(place < steps, 0.0, pltpu.roll(value, steps, axis))
    return ahead + behind


def plane_terms(plane):
    value = plane.astype(jnp.float32)
    ahead = next_in(value, 1)
    along_x = (value + ahead, ahead - value)
    shifted = [next_in(part, 0) for part in along_x]
    return [along_x[0] + shifted[0], along_x[1] + shifted[1], shifted[0] - along_x[0], shifted[1] - along_x[1]]


def add_all(values):
    values = list(values)
    while len(values) > 1:
        values = [sum(values[i : i + 2][1:], values[i]) for i in range(0, len(values), 2)]
    return values[0]


def element_form(low, high):
    squares, crosses = transformed_terms()
    wave = {}
    for component in range(3):
        for pattern in range(4):
            wave[3 * pattern + component] = low[component][pattern] + high[component][pattern]
            wave[3 * (pattern + 4) + component] = high[component][pattern] - low[component][pattern]
    stiff, by_mass = [], {}
    for (stiff_value, mass_value), rows in squares.items():
        total = add_all(wave[row] * wave[row] for row in rows)
        if stiff_value != 0.0:
            stiff.append(stiff_value * total)
        by_mass.setdefault(mass_value, []).append(total)
    for value, pairs in crosses.items():
        stiff.append(value * add_all(wave[row] * wave[column] for row, column in pairs))
    mass = [value * add_all(totals) for value, totals in by_mass.items()]
    return add_all(stiff), add_all(mass)


def filtered(near, one, two):
    def weight(square):
        return max(0.0, 2.5 - float(np.sqrt(square)))

    rings = {
        0: near,
        1: both_sides(near, 1, 0) + one,
        2: both_sides(one, 1, 0),
        4: both_sides(near, 2, 0) + two,
        5: both_sides(one, 2, 0) + both_sides(two, 1, 0),
    }

    def column(steps):
        return add_all(
            weight(square + steps * steps) * ring
            for square, ring in rings.items()
            if weight(square + steps * steps) > 0.0
        )

    return column(0) + both_sides(column(1), 1, 1) + both_sides(column(2), 2, 1)


def kernel(
    layers, groups, modes_ref, eigenvalues_ref, density_ref, out_ref,
    eigen_ref, field, upper, terms, dens, share,
    eigen_sem, field_sem, dens_sem, plane_send, plane_recv, share_send, share_recv,
):
    grid, mode = lax.axis_index("grid"), lax.axis_index("mode")
    count, depth = modes_ref.shape[0], modes_ref.shape[2]
    height, width = modes_ref.shape[3:]
    last = layers - 1

    partners = [(step, turn) for step in (-1, 1, 0) for turn in range(groups) if (step, turn) != (0, 0)]

    def target(step, turn):
        return (grid + step, lax.rem(mode + turn, groups))

    def there(step, body):
        if step < 0:
            pl.when(grid > 0)(body)
        elif step > 0:
            pl.when(grid < last)(body)
        else:
            body()

    barrier = pltpu.get_barrier_semaphore()
    for step, turn in partners:
        there(step, lambda: pl.semaphore_signal(barrier, inc=1, device_id=target(step, turn), device_id_type=MESH))

    def load(index):
        return pltpu.make_async_copy(modes_ref.at[index], field.at[index], field_sem.at[index])

    eigen_copy = pltpu.make_async_copy(eigenvalues_ref, eigen_ref, eigen_sem)
    eigen_copy.start()
    for index in range(count):
        load(index).start()
    density_copy = pltpu.make_async_copy(density_ref, dens, dens_sem)
    density_copy.start()

    sides = jnp.minimum(grid, 1) + jnp.minimum(last - grid, 1)
    pl.semaphore_wait(barrier, groups - 1 + groups * sides)

    def plane_copy(index):
        return pltpu.make_async_remote_copy(
            src_ref=modes_ref.at[index, :, 0],
            dst_ref=upper.at[index],
            send_sem=plane_send.at[index],
            recv_sem=plane_recv.at[index],
            device_id=(jnp.maximum(grid - 1, 0), mode),
            device_id_type=MESH,
        )

    @pl.when(grid > 0)
    def _():
        for index in range(count):
            plane_copy(index).start()

    @pl.when(grid == last)
    def _():
        upper[...] = jnp.zeros_like(upper)
        share[2] = jnp.zeros_like(share[2])

    @pl.when(grid == 0)
    def _():
        share[0] = jnp.zeros_like(share[0])

    ones = jnp.ones((height, width), jnp.float32)
    totals = []
    for layer in range(depth):
        place = grid * depth + layer

        def inside(steps):
            low = jnp.minimum(jnp.maximum(place - steps + 1, 0), 1)
            high = jnp.minimum(jnp.maximum(layers * depth - place - steps, 0), 1)
            return (low + high).astype(jnp.float32) * ones

        totals.append(filtered(ones, inside(1), inside(2)))

    zeros = jnp.zeros((height, width), jnp.float32)

    def first(index, carry):
        load(index).wait()
        low = [plane_terms(field[index, component, 0]) for component in range(3)]
        high = [plane_terms(field[index, component, 1]) for component in range(3)]
        for component in range(3):
            for pattern in range(4):
                terms[index, component, pattern] = high[component][pattern]
        stiff, mass = element_form(low, high)
        return carry[0] + stiff, carry[1] + eigen_ref[index] * mass

    def second(index, carry):
        @pl.when(grid < last)
        def _():
            plane_copy(index).wait_recv()

        low = [[terms[index, component, pattern] for pattern in range(4)] for component in range(3)]
        high = [plane_terms(upper[index, component]) for component in range(3)]
        stiff, mass = element_form(low, high)
        return carry[0] + stiff, carry[1] + eigen_ref[index] * mass

    def share_copy(layer, step, turn):
        return pltpu.make_async_remote_copy(
            src_ref=share.at[1, mode, layer],
            dst_ref=share.at[1 - step, mode, layer],
            send_sem=share_send.at[layer, step + 1, turn],
            recv_sem=share_recv.at[layer, 1 - step, mode],
            device_id=target(step, turn),
            device_id_type=MESH,
        )

    def arrived(layer, step, turn):
        source = lax.rem(mode + turn, groups)
        return pltpu.make_async_remote_copy(
            src_ref=share.at[1, mode, layer],
            dst_ref=share.at[1 + step, source, layer],
            send_sem=share_send.at[layer, step + 1, turn],
            recv_sem=share_recv.at[layer, 1 + step, source],
            device_id=target(step, turn),
            device_id_type=MESH,
        )

    def finish(layer, stiff, mass):
        slope = 3.0 * (1.0 - 0.001) * dens[layer] * dens[layer]
        share[1, mode, layer] = ((slope * stiff - mass) / totals[layer]).astype(jnp.bfloat16)
        for step, turn in partners:
            there(step, lambda: share_copy(layer, step, turn).start())

    eigen_copy.wait()
    stiff, mass = lax.fori_loop(0, count, first, (zeros, zeros))
    density_copy.wait()
    finish(0, stiff, mass)
    stiff, mass = lax.fori_loop(0, count, second, (zeros, zeros))
    finish(1, stiff, mass)

    for layer in range(depth):
        for step, turn in partners:
            there(step, lambda: arrived(layer, step, turn).wait_recv())

    def whole(place, layer):
        return add_all(share[place, group, layer].astype(jnp.float32) for group in range(groups))

    stack = [whole(place, layer) for place in range(3) for layer in range(depth)]
    for layer in range(depth):
        at = depth + layer
        out_ref[layer] = filtered(stack[at], stack[at - 1] + stack[at + 1], stack[at - 2] + stack[at + 2])

    for layer in range(depth):
        for step, turn in partners:
            there(step, lambda: share_copy(layer, step, turn).wait_send())

    @pl.when(grid > 0)
    def _():
        for index in range(count):
            plane_copy(index).wait_send()


def local(layers, groups, modes, eigenvalues, density):
    count, _, depth, height, width = modes.shape
    assert depth == 2
    return pl.pallas_call(
        functools.partial(kernel, layers, groups),
        out_shape=jax.ShapeDtypeStruct(density.shape, jnp.float32),
        in_specs=[
            pl.BlockSpec(memory_space=pltpu.HBM),
            pl.BlockSpec(memory_space=pltpu.HBM),
            pl.BlockSpec(memory_space=pltpu.HBM),
        ],
        out_specs=pl.BlockSpec(memory_space=pltpu.VMEM),
        scratch_shapes=[
            pltpu.SMEM(eigenvalues.shape, jnp.float32),
            pltpu.VMEM(modes.shape, jnp.bfloat16),
            pltpu.VMEM((count, 3, height, width), jnp.bfloat16),
            pltpu.VMEM((count, 3, 4, height, width), jnp.float32),
            pltpu.VMEM(density.shape, jnp.float32),
            pltpu.VMEM((3, groups, depth, height, width), jnp.bfloat16),
            pltpu.SemaphoreType.DMA,
            pltpu.SemaphoreType.DMA((count,)),
            pltpu.SemaphoreType.DMA,
            pltpu.SemaphoreType.DMA((count,)),
            pltpu.SemaphoreType.DMA((count,)),
            pltpu.SemaphoreType.DMA((depth, 3, groups)),
            pltpu.SemaphoreType.DMA((depth, 3, groups)),
        ],
        compiler_params=pltpu.CompilerParams(
            collective_id=0, has_side_effects=True, vmem_limit_bytes=60 * 1024 * 1024
        ),
        name="sensitivities",
    )(modes, eigenvalues, density)


def solution(mesh):
    in_specs = (P("mode", None, "grid", None, None), P("mode"), P("grid", None, None))
    body = functools.partial(local, mesh.shape["grid"], mesh.shape["mode"])
    return jax.shard_map(body, mesh=mesh, in_specs=in_specs, out_specs=P("grid", None, None), check_vma=False)
```

```python
import functools

import jax
import jax.numpy as jnp
import ml_dtypes
import numpy as np
from jax import lax
from jax.experimental import pallas as pl
from jax.experimental.pallas import tpu as pltpu
from jax.sharding import PartitionSpec as P

MESH = pl.DeviceIdType.MESH


def element_tables():
    poisson = 0.3
    lame_first = poisson / ((1.0 + poisson) * (1.0 - 2.0 * poisson))
    shear = 0.5 / (1.0 + poisson)
    elastic = np.zeros((6, 6))
    elastic[:3, :3] = lame_first
    for axis_bit in range(3):
        elastic[axis_bit, axis_bit] += 2.0 * shear
        elastic[axis_bit + 3, axis_bit + 3] = shear
    stiffness = np.zeros((24, 24))
    mass_small = np.zeros((8, 8))
    point = 1.0 / np.sqrt(3.0)
    for gauss in range(8):
        coords = [point * (2 * (gauss >> axis_bit & 1) - 1) for axis_bit in range(3)]
        shape_values = np.zeros(8)
        grads = np.zeros((3, 8))
        for corner in range(8):
            signs = [2 * (corner >> axis_bit & 1) - 1 for axis_bit in range(3)]
            factors = [1.0 + signs[axis_bit] * coords[axis_bit] for axis_bit in range(3)]
            shape_values[corner] = 0.125 * factors[0] * factors[1] * factors[2]
            grads[0, corner] = 0.25 * signs[0] * factors[1] * factors[2]
            grads[1, corner] = 0.25 * signs[1] * factors[0] * factors[2]
            grads[2, corner] = 0.25 * signs[2] * factors[0] * factors[1]
        strain = np.zeros((6, 24))
        for corner in range(8):
            column = 3 * corner
            strain[0, column] = grads[0, corner]
            strain[1, column + 1] = grads[1, corner]
            strain[2, column + 2] = grads[2, corner]
            strain[3, column] = grads[1, corner]
            strain[3, column + 1] = grads[0, corner]
            strain[4, column + 1] = grads[2, corner]
            strain[4, column + 2] = grads[1, corner]
            strain[5, column] = grads[2, corner]
            strain[5, column + 2] = grads[0, corner]
        stiffness = stiffness + strain.T @ elastic @ strain * 0.125
        mass_small = mass_small + np.outer(shape_values, shape_values) * 0.125
    mass = np.kron(mass_small, np.eye(3))
    return np.concatenate([stiffness, mass], 0).astype(np.float32)


def transformed_terms():
    table = element_tables().astype(ml_dtypes.bfloat16).astype(np.float64)
    change = np.ones((8, 8))
    for corner in range(8):
        for pattern in range(8):
            for bit in range(3):
                if pattern >> bit & 1 and not corner >> bit & 1:
                    change[corner, pattern] *= -1.0
    stiff, mass = (
        np.einsum("is,icjd,jt->sctd", change, part.reshape(8, 3, 8, 3), change).reshape(24, 24) / 64.0
        for part in (table[:24], table[24:])
    )
    assert np.abs(mass - np.diag(np.diag(mass))).max() < 1e-12
    squares, crosses = {}, {}
    for row in range(24):
        key = (round(stiff[row, row], 12), round(mass[row, row], 12))
        squares.setdefault(key, []).append(row)
        for column in range(row):
            value = round(stiff[row, column] + stiff[column, row], 12)
            if value != 0.0:
                crosses.setdefault(value, []).append((row, column))
    return squares, crosses


def next_in(value, axis):
    size = value.shape[axis]
    place = lax.broadcasted_iota(jnp.int32, value.shape, axis)
    return jnp.where(place == size - 1, 0.0, pltpu.roll(value, size - 1, axis))


def both_sides(value, steps, axis):
    size = value.shape[axis]
    place = lax.broadcasted_iota(jnp.int32, value.shape, axis)
    ahead = jnp.where(place >= size - steps, 0.0, pltpu.roll(value, size - steps, axis))
    behind = jnp.where(place < steps, 0.0, pltpu.roll(value, steps, axis))
    return ahead + behind


def plane_terms(plane):
    value = plane.astype(jnp.float32)
    ahead = next_in(value, 1)
    along_x = (value + ahead, ahead - value)
    shifted = [next_in(part, 0) for part in along_x]
    return [along_x[0] + shifted[0], along_x[1] + shifted[1], shifted[0] - along_x[0], shifted[1] - along_x[1]]


def add_all(values):
    values = list(values)
    while len(values) > 1:
        values = [sum(values[i : i + 2][1:], values[i]) for i in range(0, len(values), 2)]
    return values[0]


def element_form(low, high):
    squares, crosses = transformed_terms()
    wave = {}
    for component in range(3):
        for pattern in range(4):
            wave[3 * pattern + component] = low[component][pattern] + high[component][pattern]
            wave[3 * (pattern + 4) + component] = high[component][pattern] - low[component][pattern]
    stiff, by_mass = [], {}
    for (stiff_value, mass_value), rows in squares.items():
        total = add_all(wave[row] * wave[row] for row in rows)
        if stiff_value != 0.0:
            stiff.append(stiff_value * total)
        by_mass.setdefault(mass_value, []).append(total)
    for value, pairs in crosses.items():
        stiff.append(value * add_all(wave[row] * wave[column] for row, column in pairs))
    mass = [value * add_all(totals) for value, totals in by_mass.items()]
    return add_all(stiff), add_all(mass)


def filtered(near, one, two):
    def weight(square):
        return max(0.0, 2.5 - float(np.sqrt(square)))

    rings = {
        0: near,
        1: both_sides(near, 1, 0) + one,
        2: both_sides(one, 1, 0),
        4: both_sides(near, 2, 0) + two,
        5: both_sides(one, 2, 0) + both_sides(two, 1, 0),
    }

    def column(steps):
        return add_all(
            weight(square + steps * steps) * ring
            for square, ring in rings.items()
            if weight(square + steps * steps) > 0.0
        )

    return column(0) + both_sides(column(1), 1, 1) + both_sides(column(2), 2, 1)


def kernel(
    layers, groups, modes_ref, eigenvalues_ref, density_ref, out_ref,
    eigen_ref, field, upper, terms, dens, share,
    eigen_sem, field_sem, dens_sem, plane_send, plane_recv, share_send, share_recv,
):
    grid, mode = lax.axis_index("grid"), lax.axis_index("mode")
    count, depth = modes_ref.shape[0], modes_ref.shape[2]
    height, width = modes_ref.shape[3:]
    last = layers - 1

    partners = [(step, turn) for step in (-1, 1, 0) for turn in range(groups) if (step, turn) != (0, 0)]

    def target(step, turn):
        return (grid + step, lax.rem(mode + turn, groups))

    def there(step, body):
        if step < 0:
            pl.when(grid > 0)(body)
        elif step > 0:
            pl.when(grid < last)(body)
        else:
            body()

    barrier = pltpu.get_barrier_semaphore()
    for step, turn in partners:
        there(step, lambda: pl.semaphore_signal(barrier, inc=1, device_id=target(step, turn), device_id_type=MESH))

    def load(index):
        return pltpu.make_async_copy(modes_ref.at[index], field.at[index], field_sem.at[index])

    eigen_copy = pltpu.make_async_copy(eigenvalues_ref, eigen_ref, eigen_sem)
    eigen_copy.start()
    for index in range(count):
        load(index).start()
    density_copy = pltpu.make_async_copy(density_ref, dens, dens_sem)
    density_copy.start()

    sides = jnp.minimum(grid, 1) + jnp.minimum(last - grid, 1)
    pl.semaphore_wait(barrier, groups - 1 + groups * sides)

    def plane_copy(index):
        return pltpu.make_async_remote_copy(
            src_ref=modes_ref.at[index, :, 0],
            dst_ref=upper.at[index],
            send_sem=plane_send.at[index],
            recv_sem=plane_recv.at[index],
            device_id=(jnp.maximum(grid - 1, 0), mode),
            device_id_type=MESH,
        )

    @pl.when(grid > 0)
    def _():
        for index in range(count):
            plane_copy(index).start()

    @pl.when(grid == last)
    def _():
        upper[...] = jnp.zeros_like(upper)
        share[2] = jnp.zeros_like(share[2])

    @pl.when(grid == 0)
    def _():
        share[0] = jnp.zeros_like(share[0])

    ones = jnp.ones((height, width), jnp.float32)
    totals = []
    for layer in range(depth):
        place = grid * depth + layer

        def inside(steps):
            low = jnp.minimum(jnp.maximum(place - steps + 1, 0), 1)
            high = jnp.minimum(jnp.maximum(layers * depth - place - steps, 0), 1)
            return (low + high).astype(jnp.float32) * ones

        totals.append(filtered(ones, inside(1), inside(2)))

    zeros = jnp.zeros((height, width), jnp.float32)

    def first(index, carry):
        load(index).wait()
        low = [plane_terms(field[index, component, 0]) for component in range(3)]
        high = [plane_terms(field[index, component, 1]) for component in range(3)]
        for component in range(3):
            for pattern in range(4):
                terms[index, component, pattern] = high[component][pattern]
        stiff, mass = element_form(low, high)
        return carry[0] + stiff, carry[1] + eigen_ref[index] * mass

    def second(index, carry):
        @pl.when(grid < last)
        def _():
            plane_copy(index).wait_recv()

        low = [[terms[index, component, pattern] for pattern in range(4)] for component in range(3)]
        high = [plane_terms(upper[index, component]) for component in range(3)]
        stiff, mass = element_form(low, high)
        return carry[0] + stiff, carry[1] + eigen_ref[index] * mass

    def share_copy(layer, step, turn):
        return pltpu.make_async_remote_copy(
            src_ref=share.at[1, mode, layer],
            dst_ref=share.at[1 - step, mode, layer],
            send_sem=share_send.at[layer, step + 1, turn],
            recv_sem=share_recv.at[layer, 1 - step, mode],
            device_id=target(step, turn),
            device_id_type=MESH,
        )

    def arrived(layer, step, turn):
        source = lax.rem(mode + turn, groups)
        return pltpu.make_async_remote_copy(
            src_ref=share.at[1, mode, layer],
            dst_ref=share.at[1 + step, source, layer],
            send_sem=share_send.at[layer, step + 1, turn],
            recv_sem=share_recv.at[layer, 1 + step, source],
            device_id=target(step, turn),
            device_id_type=MESH,
        )

    def finish(layer, stiff, mass):
        slope = 3.0 * (1.0 - 0.001) * dens[layer] * dens[layer]
        share[1, mode, layer] = ((slope * stiff - mass) / totals[layer]).astype(jnp.bfloat16)
        for step, turn in partners:
            there(step, lambda: share_copy(layer, step, turn).start())

    eigen_copy.wait()
    stiff, mass = lax.fori_loop(0, count, first, (zeros, zeros))
    density_copy.wait()
    finish(0, stiff, mass)
    stiff, mass = lax.fori_loop(0, count, second, (zeros, zeros))
    finish(1, stiff, mass)

    for layer in range(depth):
        for step, turn in partners:
            there(step, lambda: arrived(layer, step, turn).wait_recv())

    def whole(place, layer):
        return add_all(share[place, group, layer].astype(jnp.float32) for group in range(groups))

    stack = [whole(place, layer) for place in range(3) for layer in range(depth)]
    for layer in range(depth):
        at = depth + layer
        out_ref[layer] = filtered(stack[at], stack[at - 1] + stack[at + 1], stack[at - 2] + stack[at + 2])

    for layer in range(depth):
        for step, turn in partners:
            there(step, lambda: share_copy(layer, step, turn).wait_send())

    @pl.when(grid > 0)
    def _():
        for index in range(count):
            plane_copy(index).wait_send()


def local(layers, groups, modes, eigenvalues, density):
    count, _, depth, height, width = modes.shape
    assert depth == 2
    return pl.pallas_call(
        functools.partial(kernel, layers, groups),
        out_shape=pltpu.VMEM(density.shape, jnp.float32),
        in_specs=[
            pl.BlockSpec(memory_space=pltpu.HBM),
            pl.BlockSpec(memory_space=pltpu.HBM),
            pl.BlockSpec(memory_space=pltpu.HBM),
        ],
        out_specs=pl.BlockSpec(memory_space=pltpu.VMEM),
        scratch_shapes=[
            pltpu.SMEM(eigenvalues.shape, jnp.float32),
            pltpu.VMEM(modes.shape, jnp.bfloat16),
            pltpu.VMEM((count, 3, height, width), jnp.bfloat16),
            pltpu.VMEM((count, 3, 4, height, width), jnp.float32),
            pltpu.VMEM(density.shape, jnp.float32),
            pltpu.VMEM((3, groups, depth, height, width), jnp.bfloat16),
            pltpu.SemaphoreType.DMA,
            pltpu.SemaphoreType.DMA((count,)),
            pltpu.SemaphoreType.DMA,
            pltpu.SemaphoreType.DMA((count,)),
            pltpu.SemaphoreType.DMA((count,)),
            pltpu.SemaphoreType.DMA((depth, 3, groups)),
            pltpu.SemaphoreType.DMA((depth, 3, groups)),
        ],
        compiler_params=pltpu.CompilerParams(
            collective_id=0, has_side_effects=True, vmem_limit_bytes=60 * 1024 * 1024
        ),
        name="sensitivities",
    )(modes, eigenvalues, density)


def solution(mesh):
    in_specs = (P("mode", None, "grid", None, None), P("mode"), P("grid", None, None))
    body = functools.partial(local, mesh.shape["grid"], mesh.shape["mode"])
    return jax.shard_map(body, mesh=mesh, in_specs=in_specs, out_specs=P("grid", None, None), check_vma=False)
```

```python
import functools

import jax
import jax.numpy as jnp
import ml_dtypes
import numpy as np
from jax import lax
from jax.experimental import pallas as pl
from jax.experimental.pallas import tpu as pltpu
from jax.sharding import PartitionSpec as P

MESH = pl.DeviceIdType.MESH


def element_tables():
    poisson = 0.3
    lame_first = poisson / ((1.0 + poisson) * (1.0 - 2.0 * poisson))
    shear = 0.5 / (1.0 + poisson)
    elastic = np.zeros((6, 6))
    elastic[:3, :3] = lame_first
    for axis_bit in range(3):
        elastic[axis_bit, axis_bit] += 2.0 * shear
        elastic[axis_bit + 3, axis_bit + 3] = shear
    stiffness = np.zeros((24, 24))
    mass_small = np.zeros((8, 8))
    point = 1.0 / np.sqrt(3.0)
    for gauss in range(8):
        coords = [point * (2 * (gauss >> axis_bit & 1) - 1) for axis_bit in range(3)]
        shape_values = np.zeros(8)
        grads = np.zeros((3, 8))
        for corner in range(8):
            signs = [2 * (corner >> axis_bit & 1) - 1 for axis_bit in range(3)]
            factors = [1.0 + signs[axis_bit] * coords[axis_bit] for axis_bit in range(3)]
            shape_values[corner] = 0.125 * factors[0] * factors[1] * factors[2]
            grads[0, corner] = 0.25 * signs[0] * factors[1] * factors[2]
            grads[1, corner] = 0.25 * signs[1] * factors[0] * factors[2]
            grads[2, corner] = 0.25 * signs[2] * factors[0] * factors[1]
        strain = np.zeros((6, 24))
        for corner in range(8):
            column = 3 * corner
            strain[0, column] = grads[0, corner]
            strain[1, column + 1] = grads[1, corner]
            strain[2, column + 2] = grads[2, corner]
            strain[3, column] = grads[1, corner]
            strain[3, column + 1] = grads[0, corner]
            strain[4, column + 1] = grads[2, corner]
            strain[4, column + 2] = grads[1, corner]
            strain[5, column] = grads[2, corner]
            strain[5, column + 2] = grads[0, corner]
        stiffness = stiffness + strain.T @ elastic @ strain * 0.125
        mass_small = mass_small + np.outer(shape_values, shape_values) * 0.125
    mass = np.kron(mass_small, np.eye(3))
    return np.concatenate([stiffness, mass], 0).astype(np.float32)


def transformed_terms():
    table = element_tables().astype(ml_dtypes.bfloat16).astype(np.float64)
    change = np.ones((8, 8))
    for corner in range(8):
        for pattern in range(8):
            for bit in range(3):
                if pattern >> bit & 1 and not corner >> bit & 1:
                    change[corner, pattern] *= -1.0
    stiff, mass = (
        np.einsum("is,icjd,jt->sctd", change, part.reshape(8, 3, 8, 3), change).reshape(24, 24) / 64.0
        for part in (table[:24], table[24:])
    )
    assert np.abs(mass - np.diag(np.diag(mass))).max() < 1e-12
    squares, crosses = {}, {}
    for row in range(24):
        key = (round(stiff[row, row], 12), round(mass[row, row], 12))
        squares.setdefault(key, []).append(row)
        for column in range(row):
            value = round(stiff[row, column] + stiff[column, row], 12)
            if value != 0.0:
                crosses.setdefault(value, []).append((row, column))
    return squares, crosses


def next_in(value, axis):
    size = value.shape[axis]
    place = lax.broadcasted_iota(jnp.int32, value.shape, axis)
    return jnp.where(place == size - 1, 0.0, pltpu.roll(value, size - 1, axis))


def both_sides(value, steps, axis):
    size = value.shape[axis]
    place = lax.broadcasted_iota(jnp.int32, value.shape, axis)
    ahead = jnp.where(place >= size - steps, 0.0, pltpu.roll(value, size - steps, axis))
    behind = jnp.where(place < steps, 0.0, pltpu.roll(value, steps, axis))
    return ahead + behind


def plane_terms(plane):
    value = plane.astype(jnp.float32)
    ahead = next_in(value, 1)
    along_x = (value + ahead, ahead - value)
    shifted = [next_in(part, 0) for part in along_x]
    return [along_x[0] + shifted[0], along_x[1] + shifted[1], shifted[0] - along_x[0], shifted[1] - along_x[1]]


def add_all(values):
    values = list(values)
    while len(values) > 1:
        values = [sum(values[i : i + 2][1:], values[i]) for i in range(0, len(values), 2)]
    return values[0]


def element_form(low, high):
    squares, crosses = transformed_terms()
    wave = {}
    for component in range(3):
        for pattern in range(4):
            wave[3 * pattern + component] = low[component][pattern] + high[component][pattern]
            wave[3 * (pattern + 4) + component] = high[component][pattern] - low[component][pattern]
    stiff, by_mass = [], {}
    for (stiff_value, mass_value), rows in squares.items():
        total = add_all(wave[row] * wave[row] for row in rows)
        if stiff_value != 0.0:
            stiff.append(stiff_value * total)
        by_mass.setdefault(mass_value, []).append(total)
    for value, pairs in crosses.items():
        stiff.append(value * add_all(wave[row] * wave[column] for row, column in pairs))
    mass = [value * add_all(totals) for value, totals in by_mass.items()]
    return add_all(stiff), add_all(mass)


def ring_columns(near, one, two):
    def weight(square):
        return max(0.0, 2.5 - float(np.sqrt(square)))

    rings = []
    for square, layer in ((0, near), (1, one), (4, two)):
        if layer is not None:
            rings.append((square, layer))
            for steps in (1, 2):
                if weight(square + steps * steps) > 0.0:
                    rings.append((square + steps * steps, both_sides(layer, steps, 0)))
    gathered = {}
    for square, ring in rings:
        gathered.setdefault(square, []).append(ring)
    gathered = {square: add_all(parts) for square, parts in gathered.items()}
    return [
        add_all(
            weight(square + steps * steps) * ring
            for square, ring in gathered.items()
            if weight(square + steps * steps) > 0.0
        )
        for steps in range(3)
    ]


def along_rows(columns):
    return columns[0] + both_sides(columns[1], 1, 1) + both_sides(columns[2], 2, 1)


def kernel(
    layers, groups, modes_ref, eigenvalues_ref, density_ref, out_ref,
    eigen_ref, field, upper, terms, dens, share,
    eigen_sem, field_sem, dens_sem, plane_send, plane_recv, share_send, share_recv,
):
    grid, mode = lax.axis_index("grid"), lax.axis_index("mode")
    count, depth = modes_ref.shape[0], modes_ref.shape[2]
    height, width = modes_ref.shape[3:]
    last = layers - 1

    partners = [(step, turn) for step in (-1, 1, 0) for turn in range(groups) if (step, turn) != (0, 0)]

    def target(step, turn):
        return (grid + step, lax.rem(mode + turn, groups))

    def there(step, body):
        if step < 0:
            pl.when(grid > 0)(body)
        elif step > 0:
            pl.when(grid < last)(body)
        else:
            body()

    barrier = pltpu.get_barrier_semaphore()
    for step, turn in partners:
        there(step, lambda: pl.semaphore_signal(barrier, inc=1, device_id=target(step, turn), device_id_type=MESH))

    def load(index):
        return pltpu.make_async_copy(modes_ref.at[index], field.at[index], field_sem.at[index])

    eigen_copy = pltpu.make_async_copy(eigenvalues_ref, eigen_ref, eigen_sem)
    eigen_copy.start()
    for index in range(count):
        load(index).start()
    density_copy = pltpu.make_async_copy(density_ref, dens, dens_sem)
    density_copy.start()

    @pl.when(grid == last)
    def _():
        upper[...] = jnp.zeros_like(upper)
        share[2] = jnp.zeros_like(share[2])

    @pl.when(grid == 0)
    def _():
        share[0] = jnp.zeros_like(share[0])

    ones = jnp.ones((height, width), jnp.float32)
    totals = []
    for layer in range(depth):
        place = grid * depth + layer

        def inside(steps):
            low = jnp.minimum(jnp.maximum(place - steps + 1, 0), 1)
            high = jnp.minimum(jnp.maximum(layers * depth - place - steps, 0), 1)
            return (low + high).astype(jnp.float32) * ones

        totals.append(along_rows(ring_columns(ones, inside(1), inside(2))))

    sides = jnp.minimum(grid, 1) + jnp.minimum(last - grid, 1)
    pl.semaphore_wait(barrier, groups - 1 + groups * sides)

    def plane_copy(index):
        return pltpu.make_async_remote_copy(
            src_ref=modes_ref.at[index, :, 0],
            dst_ref=upper.at[index],
            send_sem=plane_send.at[index],
            recv_sem=plane_recv.at[index],
            device_id=(jnp.maximum(grid - 1, 0), mode),
            device_id_type=MESH,
        )

    @pl.when(grid > 0)
    def _():
        for index in range(count):
            plane_copy(index).start()

    zeros = jnp.zeros((height, width), jnp.float32)

    def first(index, carry):
        load(index).wait()
        low = [plane_terms(field[index, component, 0]) for component in range(3)]
        high = [plane_terms(field[index, component, 1]) for component in range(3)]
        for component in range(3):
            for pattern in range(4):
                terms[index, component, pattern] = high[component][pattern]
        stiff, mass = element_form(low, high)
        return carry[0] + stiff, carry[1] + eigen_ref[index] * mass

    def second(index, carry):
        @pl.when(grid < last)
        def _():
            plane_copy(index).wait_recv()

        low = [[terms[index, component, pattern] for pattern in range(4)] for component in range(3)]
        high = [plane_terms(upper[index, component]) for component in range(3)]
        stiff, mass = element_form(low, high)
        return carry[0] + stiff, carry[1] + eigen_ref[index] * mass

    def share_copy(layer, step, turn):
        return pltpu.make_async_remote_copy(
            src_ref=share.at[1, mode, layer],
            dst_ref=share.at[1 - step, mode, layer],
            send_sem=share_send.at[layer, step + 1, turn],
            recv_sem=share_recv.at[layer, 1 - step, mode],
            device_id=target(step, turn),
            device_id_type=MESH,
        )

    def arrived(layer, step, turn):
        source = lax.rem(mode + turn, groups)
        return pltpu.make_async_remote_copy(
            src_ref=share.at[1, mode, layer],
            dst_ref=share.at[1 + step, source, layer],
            send_sem=share_send.at[layer, step + 1, turn],
            recv_sem=share_recv.at[layer, 1 + step, source],
            device_id=target(step, turn),
            device_id_type=MESH,
        )

    def finish(layer, stiff, mass):
        slope = 3.0 * (1.0 - 0.001) * dens[layer] * dens[layer]
        share[1, mode, layer] = ((slope * stiff - mass) / totals[layer]).astype(jnp.bfloat16)
        for step, turn in partners:
            there(step, lambda: share_copy(layer, step, turn).start())

    eigen_copy.wait()
    stiff, mass = lax.fori_loop(0, count, first, (zeros, zeros))
    density_copy.wait()
    finish(0, stiff, mass)
    stiff, mass = lax.fori_loop(0, count, second, (zeros, zeros))
    finish(1, stiff, mass)

    def whole(place, layer):
        return add_all(share[place, group, layer].astype(jnp.float32) for group in range(groups))

    def await_layer(layer):
        for step, turn in reversed(partners):
            there(step, lambda: arrived(layer, step, turn).wait_recv())
        return [whole(place, layer) for place in range(3)]

    below, centre, above = await_layer(0)
    early = [ring_columns(centre, None, below + above), ring_columns(None, centre + above, None)]
    below, centre, above = await_layer(1)
    late = [ring_columns(None, below + centre, None), ring_columns(centre, None, below + above)]
    for layer in range(depth):
        out_ref[layer] = along_rows([one + two for one, two in zip(early[layer], late[layer])])

    for layer in range(depth):
        for step, turn in partners:
            there(step, lambda: share_copy(layer, step, turn).wait_send())

    @pl.when(grid > 0)
    def _():
        for index in range(count):
            plane_copy(index).wait_send()


def local(layers, groups, modes, eigenvalues, density):
    count, _, depth, height, width = modes.shape
    assert depth == 2
    return pl.pallas_call(
        functools.partial(kernel, layers, groups),
        out_shape=pltpu.VMEM(density.shape, jnp.float32),
        in_specs=[
            pl.BlockSpec(memory_space=pltpu.HBM),
            pl.BlockSpec(memory_space=pltpu.HBM),
            pl.BlockSpec(memory_space=pltpu.HBM),
        ],
        out_specs=pl.BlockSpec(memory_space=pltpu.VMEM),
        scratch_shapes=[
            pltpu.SMEM(eigenvalues.shape, jnp.float32),
            pltpu.VMEM(modes.shape, jnp.bfloat16),
            pltpu.VMEM((count, 3, height, width), jnp.bfloat16),
            pltpu.VMEM((count, 3, 4, height, width), jnp.float32),
            pltpu.VMEM(density.shape, jnp.float32),
            pltpu.VMEM((3, groups, depth, height, width), jnp.bfloat16),
            pltpu.SemaphoreType.DMA,
            pltpu.SemaphoreType.DMA((count,)),
            pltpu.SemaphoreType.DMA,
            pltpu.SemaphoreType.DMA((count,)),
            pltpu.SemaphoreType.DMA((count,)),
            pltpu.SemaphoreType.DMA((depth, 3, groups)),
            pltpu.SemaphoreType.DMA((depth, 3, groups)),
        ],
        compiler_params=pltpu.CompilerParams(
            collective_id=0, has_side_effects=True, vmem_limit_bytes=60 * 1024 * 1024
        ),
        name="sensitivities",
    )(modes, eigenvalues, density)


def solution(mesh):
    in_specs = (P("mode", None, "grid", None, None), P("mode"), P("grid", None, None))
    body = functools.partial(local, mesh.shape["grid"], mesh.shape["mode"])
    return jax.shard_map(body, mesh=mesh, in_specs=in_specs, out_specs=P("grid", None, None), check_vma=False)
```

```python
import functools

import jax
import jax.numpy as jnp
import ml_dtypes
import numpy as np
from jax import lax
from jax.experimental import pallas as pl
from jax.experimental.pallas import tpu as pltpu
from jax.sharding import PartitionSpec as P

MESH = pl.DeviceIdType.MESH


def element_tables():
    poisson = 0.3
    lame_first = poisson / ((1.0 + poisson) * (1.0 - 2.0 * poisson))
    shear = 0.5 / (1.0 + poisson)
    elastic = np.zeros((6, 6))
    elastic[:3, :3] = lame_first
    for axis_bit in range(3):
        elastic[axis_bit, axis_bit] += 2.0 * shear
        elastic[axis_bit + 3, axis_bit + 3] = shear
    stiffness = np.zeros((24, 24))
    mass_small = np.zeros((8, 8))
    point = 1.0 / np.sqrt(3.0)
    for gauss in range(8):
        coords = [point * (2 * (gauss >> axis_bit & 1) - 1) for axis_bit in range(3)]
        shape_values = np.zeros(8)
        grads = np.zeros((3, 8))
        for corner in range(8):
            signs = [2 * (corner >> axis_bit & 1) - 1 for axis_bit in range(3)]
            factors = [1.0 + signs[axis_bit] * coords[axis_bit] for axis_bit in range(3)]
            shape_values[corner] = 0.125 * factors[0] * factors[1] * factors[2]
            grads[0, corner] = 0.25 * signs[0] * factors[1] * factors[2]
            grads[1, corner] = 0.25 * signs[1] * factors[0] * factors[2]
            grads[2, corner] = 0.25 * signs[2] * factors[0] * factors[1]
        strain = np.zeros((6, 24))
        for corner in range(8):
            column = 3 * corner
            strain[0, column] = grads[0, corner]
            strain[1, column + 1] = grads[1, corner]
            strain[2, column + 2] = grads[2, corner]
            strain[3, column] = grads[1, corner]
            strain[3, column + 1] = grads[0, corner]
            strain[4, column + 1] = grads[2, corner]
            strain[4, column + 2] = grads[1, corner]
            strain[5, column] = grads[2, corner]
            strain[5, column + 2] = grads[0, corner]
        stiffness = stiffness + strain.T @ elastic @ strain * 0.125
        mass_small = mass_small + np.outer(shape_values, shape_values) * 0.125
    mass = np.kron(mass_small, np.eye(3))
    return np.concatenate([stiffness, mass], 0).astype(np.float32)


def transformed_terms():
    table = element_tables().astype(ml_dtypes.bfloat16).astype(np.float64)
    change = np.ones((8, 8))
    for corner in range(8):
        for pattern in range(8):
            for bit in range(3):
                if pattern >> bit & 1 and not corner >> bit & 1:
                    change[corner, pattern] *= -1.0
    stiff, mass = (
        np.einsum("is,icjd,jt->sctd", change, part.reshape(8, 3, 8, 3), change).reshape(24, 24) / 64.0
        for part in (table[:24], table[24:])
    )
    assert np.abs(mass - np.diag(np.diag(mass))).max() < 1e-12
    squares, crosses = {}, {}
    for row in range(24):
        key = (round(stiff[row, row], 12), round(mass[row, row], 12))
        squares.setdefault(key, []).append(row)
        for column in range(row):
            value = round(stiff[row, column] + stiff[column, row], 12)
            if value != 0.0:
                crosses.setdefault(value, []).append((row, column))
    return squares, crosses


def next_in(value, axis):
    size = value.shape[axis]
    place = lax.broadcasted_iota(jnp.int32, value.shape, axis)
    return jnp.where(place == size - 1, 0.0, pltpu.roll(value, size - 1, axis))


def both_sides(value, steps, axis):
    size = value.shape[axis]
    place = lax.broadcasted_iota(jnp.int32, value.shape, axis)
    ahead = jnp.where(place >= size - steps, 0.0, pltpu.roll(value, size - steps, axis))
    behind = jnp.where(place < steps, 0.0, pltpu.roll(value, steps, axis))
    return ahead + behind


def plane_terms(plane):
    value = plane.astype(jnp.float32)
    ahead = next_in(value, 1)
    along_x = (value + ahead, ahead - value)
    shifted = [next_in(part, 0) for part in along_x]
    return [along_x[0] + shifted[0], along_x[1] + shifted[1], shifted[0] - along_x[0], shifted[1] - along_x[1]]


def add_all(values):
    values = list(values)
    while len(values) > 1:
        values = [sum(values[i : i + 2][1:], values[i]) for i in range(0, len(values), 2)]
    return values[0]


def element_form(low, high):
    squares, crosses = transformed_terms()
    wave = {}
    for component in range(3):
        for pattern in range(4):
            wave[3 * pattern + component] = low[component][pattern] + high[component][pattern]
            wave[3 * (pattern + 4) + component] = high[component][pattern] - low[component][pattern]
    stiff, by_mass = [], {}
    for (stiff_value, mass_value), rows in squares.items():
        total = add_all(wave[row] * wave[row] for row in rows)
        if stiff_value != 0.0:
            stiff.append(stiff_value * total)
        by_mass.setdefault(mass_value, []).append(total)
    for value, pairs in crosses.items():
        stiff.append(value * add_all(wave[row] * wave[column] for row, column in pairs))
    mass = [value * add_all(totals) for value, totals in by_mass.items()]
    return add_all(stiff), add_all(mass)


def ring_columns(near, one, two):
    def weight(square):
        return max(0.0, 2.5 - float(np.sqrt(square)))

    rings = []
    for square, layer in ((0, near), (1, one), (4, two)):
        if layer is not None:
            rings.append((square, layer))
            for steps in (1, 2):
                if weight(square + steps * steps) > 0.0:
                    rings.append((square + steps * steps, both_sides(layer, steps, 0)))
    gathered = {}
    for square, ring in rings:
        gathered.setdefault(square, []).append(ring)
    gathered = {square: add_all(parts) for square, parts in gathered.items()}
    return [
        add_all(
            weight(square + steps * steps) * ring
            for square, ring in gathered.items()
            if weight(square + steps * steps) > 0.0
        )
        for steps in range(3)
    ]


def along_rows(columns):
    return columns[0] + both_sides(columns[1], 1, 1) + both_sides(columns[2], 2, 1)


def kernel(
    layers, groups, modes_ref, eigenvalues_ref, density_ref, out_ref,
    eigen_ref, field, upper, terms, dens, share, sums,
    eigen_sem, field_sem, dens_sem, plane_send, plane_recv, share_send, share_recv,
):
    grid, mode = lax.axis_index("grid"), lax.axis_index("mode")
    count, depth = modes_ref.shape[0], modes_ref.shape[2]
    height, width = modes_ref.shape[3:]
    last = layers - 1

    partners = [(step, turn) for step in (-2, 2, -1, 1, 0) for turn in range(groups) if (step, turn) != (0, 0)]
    half = count // 2

    def target(step, turn):
        return (grid + step, lax.rem(mode + turn, groups))

    def there(step, body):
        if step < 0:
            pl.when(grid + step >= 0)(body)
        elif step > 0:
            pl.when(grid + step <= last)(body)
        else:
            body()

    barrier = pltpu.get_barrier_semaphore()
    for step, turn in partners:
        there(step, lambda: pl.semaphore_signal(barrier, inc=1, device_id=target(step, turn), device_id_type=MESH))

    def load(index):
        return pltpu.make_async_copy(modes_ref.at[index], field.at[index], field_sem.at[index])

    eigen_copy = pltpu.make_async_copy(eigenvalues_ref, eigen_ref, eigen_sem)
    eigen_copy.start()
    for index in range(count):
        load(index).start()
    density_copy = pltpu.make_async_copy(density_ref, dens.at[:depth], dens_sem)
    density_copy.start()

    @pl.when(grid == last)
    def _():
        upper[:half] = jnp.zeros_like(upper[:half])
        share[0, 2] = jnp.zeros_like(share[0, 2])
        share[1, 2] = jnp.zeros_like(share[1, 2])
        share[2, 1] = jnp.zeros_like(share[2, 1])

    @pl.when(grid >= last - 1)
    def _():
        share[2, 2] = jnp.zeros_like(share[2, 2])

    @pl.when(grid == 0)
    def _():
        share[0, 0] = jnp.zeros_like(share[0, 0])
        share[1, 0] = jnp.zeros_like(share[1, 0])
        share[2, 0] = jnp.zeros_like(share[2, 0])

    ones = jnp.ones((height, width), jnp.float32)
    totals = []
    for layer in (0, 1, -1):
        place = grid * depth + layer

        def inside(steps):
            low = jnp.minimum(jnp.maximum(place - steps + 1, 0), 1)
            high = jnp.minimum(jnp.maximum(layers * depth - place - steps, 0), 1)
            return (low + high).astype(jnp.float32) * ones

        totals.append(along_rows(ring_columns(ones, inside(1), inside(2))))

    sides = jnp.minimum(grid, 2) + jnp.minimum(last - grid, 2)
    pl.semaphore_wait(barrier, groups - 1 + groups * sides)

    def plane_copy(index):
        up = index >= half
        return pltpu.make_async_remote_copy(
            src_ref=modes_ref.at[index, :, depth - 1 if up else 0],
            dst_ref=upper.at[index],
            send_sem=plane_send.at[index],
            recv_sem=plane_recv.at[index],
            device_id=target(1 if up else -1, 0),
            device_id_type=MESH,
        )

    def density_up():
        return pltpu.make_async_remote_copy(
            src_ref=density_ref.at[depth - 1],
            dst_ref=dens.at[depth],
            send_sem=plane_send.at[count],
            recv_sem=plane_recv.at[count],
            device_id=target(1, 0),
            device_id_type=MESH,
        )

    def arriving(index):
        return pltpu.make_async_remote_copy(
            src_ref=modes_ref.at[index, :, 0],
            dst_ref=upper.at[index],
            send_sem=plane_send.at[index],
            recv_sem=plane_recv.at[index],
            device_id=target(0, 0),
            device_id_type=MESH,
        )

    down, up = range(half), range(half, count)
    for one, two in zip(down, up):
        there(-1, lambda: plane_copy(one).start())
        there(1, lambda: plane_copy(two).start())
    there(1, lambda: density_up().start())

    zeros = jnp.zeros((height, width), jnp.float32)

    def first(index, carry):
        load(index).wait()
        low = [plane_terms(field[index, component, 0]) for component in range(3)]
        high = [plane_terms(field[index, component, 1]) for component in range(3)]
        kept = jnp.where(index < half, 1.0, 0.0)
        for component in range(3):
            for pattern in range(4):
                top, bottom = high[component][pattern], low[component][pattern]
                terms[index, component, pattern] = kept * top + (1.0 - kept) * bottom
        stiff, mass = element_form(low, high)
        return carry[0] + stiff, carry[1] + eigen_ref[index] * mass

    def kept_terms(index):
        return [[terms[index, component, pattern] for pattern in range(4)] for component in range(3)]

    def add_form(layer, index, low, high):
        stiff, mass = element_form(low, high)
        sums[layer, 0] += stiff
        sums[layer, 1] += eigen_ref[index] * mass

    reach = {0: (-1, 1, 0), 1: (-1, 1, 0), 2: (-2, -1, 0)}

    def sends(kind):
        return [(step, turn) for step in reach[kind] for turn in range(groups) if (step, turn) != (0, 0)]

    def slot(kind, source):
        return source if kind == 2 else source + 1

    def share_copy(kind, step, turn):
        return pltpu.make_async_remote_copy(
            src_ref=share.at[kind, slot(kind, 0), mode],
            dst_ref=share.at[kind, slot(kind, -step), mode],
            send_sem=share_send.at[kind, slot(kind, -step), turn],
            recv_sem=share_recv.at[kind, slot(kind, -step), mode],
            device_id=target(step, turn),
            device_id_type=MESH,
        )

    def arrived(kind, source, turn):
        group = lax.rem(mode + turn, groups)
        return pltpu.make_async_remote_copy(
            src_ref=share.at[kind, slot(kind, 0), mode],
            dst_ref=share.at[kind, slot(kind, source), group],
            send_sem=share_send.at[kind, slot(kind, source), turn],
            recv_sem=share_recv.at[kind, slot(kind, source), group],
            device_id=target(0, 0),
            device_id_type=MESH,
        )

    def finish(kind, density, stiff, mass):
        slope = 3.0 * (1.0 - 0.001) * density * density
        share[kind, slot(kind, 0), mode] = ((slope * stiff - mass) / totals[kind]).astype(jnp.bfloat16)
        for step, turn in sends(kind):
            there(step, lambda: share_copy(kind, step, turn).start())

    eigen_copy.wait()
    stiff, mass = lax.fori_loop(0, count, first, (zeros, zeros))
    density_copy.wait()
    finish(0, dens[0], stiff, mass)
    sums[...] = jnp.zeros_like(sums)

    @pl.when(grid == last)
    def _():
        @pl.loop(half, count)
        def _(index):
            low = [plane_terms(field[index, component, 1]) for component in range(3)]
            add_form(0, index, low, [[zeros] * 4] * 3)

    @pl.loop(0, half)
    def _(index):
        @pl.when(grid < last)
        def _():
            arriving(index).wait_recv()

        add_form(0, index, kept_terms(index), [plane_terms(upper[index, component]) for component in range(3)])

    finish(1, dens[1], sums[0, 0], sums[0, 1])

    @pl.when(grid > 0)
    def _():
        @pl.loop(half, count)
        def _(index):
            arriving(index).wait_recv()
            add_form(1, index, [plane_terms(upper[index, component]) for component in range(3)], kept_terms(index))

        density_up().wait_recv()
        finish(2, dens[depth], sums[1, 0], sums[1, 1])

    def whole(kind, place):
        return add_all(share[kind, place, group].astype(jnp.float32) for group in range(groups))

    def await_kind(kind):
        for step, turn in reversed(sends(kind)):
            pair = functools.partial(there, -step)
            body = lambda: arrived(kind, -step, turn).wait_recv()
            if kind == 2 and step == 0:
                pl.when(grid > 0)(body)
            else:
                pair(body)
        return [whole(kind, place) for place in range(3)]

    below, centre, above = await_kind(0)
    early = [ring_columns(centre, None, below + above), ring_columns(None, centre + above, None)]
    below, centre, above = [one + two for one, two in zip(await_kind(1), await_kind(2))]
    late = [ring_columns(None, below + centre, None), ring_columns(centre, None, below + above)]
    for layer in range(depth):
        out_ref[layer] = along_rows([one + two for one, two in zip(early[layer], late[layer])])

    for kind in range(3):
        for step, turn in sends(kind):
            body = lambda: share_copy(kind, step, turn).wait_send()
            if kind == 2 and step == 0:
                pl.when(grid > 0)(body)
            else:
                there(step, body)
    for one, two in zip(down, up):
        there(-1, lambda: plane_copy(one).wait_send())
        there(1, lambda: plane_copy(two).wait_send())
    there(1, lambda: density_up().wait_send())


def local(layers, groups, modes, eigenvalues, density):
    count, _, depth, height, width = modes.shape
    assert depth == 2 and count % 2 == 0
    return pl.pallas_call(
        functools.partial(kernel, layers, groups),
        out_shape=pltpu.VMEM(density.shape, jnp.float32),
        in_specs=[
            pl.BlockSpec(memory_space=pltpu.HBM),
            pl.BlockSpec(memory_space=pltpu.HBM),
            pl.BlockSpec(memory_space=pltpu.HBM),
        ],
        out_specs=pl.BlockSpec(memory_space=pltpu.VMEM),
        scratch_shapes=[
            pltpu.SMEM(eigenvalues.shape, jnp.float32),
            pltpu.VMEM(modes.shape, jnp.bfloat16),
            pltpu.VMEM((count, 3, height, width), jnp.bfloat16),
            pltpu.VMEM((count, 3, 4, height, width), jnp.float32),
            pltpu.VMEM((depth + 1, height, width), jnp.float32),
            pltpu.VMEM((3, 3, groups, height, width), jnp.bfloat16),
            pltpu.VMEM((2, 2, height, width), jnp.float32),
            pltpu.SemaphoreType.DMA,
            pltpu.SemaphoreType.DMA((count,)),
            pltpu.SemaphoreType.DMA,
            pltpu.SemaphoreType.DMA((count + 1,)),
            pltpu.SemaphoreType.DMA((count + 1,)),
            pltpu.SemaphoreType.DMA((3, 3, groups)),
            pltpu.SemaphoreType.DMA((3, 3, groups)),
        ],
        compiler_params=pltpu.CompilerParams(
            collective_id=0, has_side_effects=True, vmem_limit_bytes=60 * 1024 * 1024
        ),
        name="sensitivities",
    )(modes, eigenvalues, density)


def solution(mesh):
    in_specs = (P("mode", None, "grid", None, None), P("mode"), P("grid", None, None))
    body = functools.partial(local, mesh.shape["grid"], mesh.shape["mode"])
    return jax.shard_map(body, mesh=mesh, in_specs=in_specs, out_specs=P("grid", None, None), check_vma=False)
```

```python
import functools

import jax
import jax.numpy as jnp
import ml_dtypes
import numpy as np
from jax import lax
from jax.experimental import pallas as pl
from jax.experimental.pallas import tpu as pltpu
from jax.sharding import PartitionSpec as P

MESH = pl.DeviceIdType.MESH


def element_tables():
    poisson = 0.3
    lame_first = poisson / ((1.0 + poisson) * (1.0 - 2.0 * poisson))
    shear = 0.5 / (1.0 + poisson)
    elastic = np.zeros((6, 6))
    elastic[:3, :3] = lame_first
    for axis_bit in range(3):
        elastic[axis_bit, axis_bit] += 2.0 * shear
        elastic[axis_bit + 3, axis_bit + 3] = shear
    stiffness = np.zeros((24, 24))
    mass_small = np.zeros((8, 8))
    point = 1.0 / np.sqrt(3.0)
    for gauss in range(8):
        coords = [point * (2 * (gauss >> axis_bit & 1) - 1) for axis_bit in range(3)]
        shape_values = np.zeros(8)
        grads = np.zeros((3, 8))
        for corner in range(8):
            signs = [2 * (corner >> axis_bit & 1) - 1 for axis_bit in range(3)]
            factors = [1.0 + signs[axis_bit] * coords[axis_bit] for axis_bit in range(3)]
            shape_values[corner] = 0.125 * factors[0] * factors[1] * factors[2]
            grads[0, corner] = 0.25 * signs[0] * factors[1] * factors[2]
            grads[1, corner] = 0.25 * signs[1] * factors[0] * factors[2]
            grads[2, corner] = 0.25 * signs[2] * factors[0] * factors[1]
        strain = np.zeros((6, 24))
        for corner in range(8):
            column = 3 * corner
            strain[0, column] = grads[0, corner]
            strain[1, column + 1] = grads[1, corner]
            strain[2, column + 2] = grads[2, corner]
            strain[3, column] = grads[1, corner]
            strain[3, column + 1] = grads[0, corner]
            strain[4, column + 1] = grads[2, corner]
            strain[4, column + 2] = grads[1, corner]
            strain[5, column] = grads[2, corner]
            strain[5, column + 2] = grads[0, corner]
        stiffness = stiffness + strain.T @ elastic @ strain * 0.125
        mass_small = mass_small + np.outer(shape_values, shape_values) * 0.125
    mass = np.kron(mass_small, np.eye(3))
    return np.concatenate([stiffness, mass], 0).astype(np.float32)


def transformed_terms():
    table = element_tables().astype(ml_dtypes.bfloat16).astype(np.float64)
    change = np.ones((8, 8))
    for corner in range(8):
        for pattern in range(8):
            for bit in range(3):
                if pattern >> bit & 1 and not corner >> bit & 1:
                    change[corner, pattern] *= -1.0
    stiff, mass = (
        np.einsum("is,icjd,jt->sctd", change, part.reshape(8, 3, 8, 3), change).reshape(24, 24) / 64.0
        for part in (table[:24], table[24:])
    )
    assert np.abs(mass - np.diag(np.diag(mass))).max() < 1e-12
    squares, crosses = {}, {}
    for row in range(24):
        key = (round(stiff[row, row], 12), round(mass[row, row], 12))
        squares.setdefault(key, []).append(row)
        for column in range(row):
            value = round(stiff[row, column] + stiff[column, row], 12)
            if value != 0.0:
                crosses.setdefault(value, []).append((row, column))
    return squares, crosses


def next_in(value, axis):
    size = value.shape[axis]
    place = lax.broadcasted_iota(jnp.int32, value.shape, axis)
    return jnp.where(place == size - 1, 0.0, pltpu.roll(value, size - 1, axis))


def both_sides(value, steps, axis):
    size = value.shape[axis]
    place = lax.broadcasted_iota(jnp.int32, value.shape, axis)
    ahead = jnp.where(place >= size - steps, 0.0, pltpu.roll(value, size - steps, axis))
    behind = jnp.where(place < steps, 0.0, pltpu.roll(value, steps, axis))
    return ahead + behind


def plane_terms(plane):
    value = plane.astype(jnp.float32)
    ahead = next_in(value, 1)
    along_x = (value + ahead, ahead - value)
    shifted = [next_in(part, 0) for part in along_x]
    return [along_x[0] + shifted[0], along_x[1] + shifted[1], shifted[0] - along_x[0], shifted[1] - along_x[1]]


def add_all(values):
    values = list(values)
    while len(values) > 1:
        values = [sum(values[i : i + 2][1:], values[i]) for i in range(0, len(values), 2)]
    return values[0]


def element_form(low, high):
    squares, crosses = transformed_terms()
    wave = {}
    for component in range(3):
        for pattern in range(4):
            wave[3 * pattern + component] = low[component][pattern] + high[component][pattern]
            wave[3 * (pattern + 4) + component] = high[component][pattern] - low[component][pattern]
    stiff, by_mass = [], {}
    for (stiff_value, mass_value), rows in squares.items():
        total = add_all(wave[row] * wave[row] for row in rows)
        if stiff_value != 0.0:
            stiff.append(stiff_value * total)
        by_mass.setdefault(mass_value, []).append(total)
    for value, pairs in crosses.items():
        stiff.append(value * add_all(wave[row] * wave[column] for row, column in pairs))
    mass = [value * add_all(totals) for value, totals in by_mass.items()]
    return add_all(stiff), add_all(mass)


def ring_columns(near, one, two):
    def weight(square):
        return max(0.0, 2.5 - float(np.sqrt(square)))

    rings = []
    for square, layer in ((0, near), (1, one), (4, two)):
        if layer is not None:
            rings.append((square, layer))
            for steps in (1, 2):
                if weight(square + steps * steps) > 0.0:
                    rings.append((square + steps * steps, both_sides(layer, steps, 0)))
    gathered = {}
    for square, ring in rings:
        gathered.setdefault(square, []).append(ring)
    gathered = {square: add_all(parts) for square, parts in gathered.items()}
    return [
        add_all(
            weight(square + steps * steps) * ring
            for square, ring in gathered.items()
            if weight(square + steps * steps) > 0.0
        )
        for steps in range(3)
    ]


def along_rows(columns):
    return columns[0] + both_sides(columns[1], 1, 1) + both_sides(columns[2], 2, 1)


def kernel(
    layers, groups, modes_ref, eigenvalues_ref, density_ref, out_ref,
    eigen_ref, field, upper, terms, dens, share, sums,
    eigen_sem, field_sem, dens_sem, plane_send, plane_recv, share_send, share_recv,
):
    grid, mode = lax.axis_index("grid"), lax.axis_index("mode")
    count, depth = modes_ref.shape[0], modes_ref.shape[2]
    height, width = modes_ref.shape[3:]
    last = layers - 1

    partners = [(step, turn) for step in (-2, 2, -1, 1, 0) for turn in range(groups) if (step, turn) != (0, 0)]
    half = count // 2

    def target(step, turn):
        return (grid + step, lax.rem(mode + turn, groups))

    def there(step, body):
        if step < 0:
            pl.when(grid + step >= 0)(body)
        elif step > 0:
            pl.when(grid + step <= last)(body)
        else:
            body()

    barrier = pltpu.get_barrier_semaphore()
    for step, turn in partners:
        there(step, lambda: pl.semaphore_signal(barrier, inc=1, device_id=target(step, turn), device_id_type=MESH))

    def load(index):
        return pltpu.make_async_copy(modes_ref.at[index], field.at[index], field_sem.at[index])

    eigen_copy = pltpu.make_async_copy(eigenvalues_ref, eigen_ref, eigen_sem)
    eigen_copy.start()
    for index in range(count):
        load(index).start()
    density_copy = pltpu.make_async_copy(density_ref, dens.at[:depth], dens_sem)
    density_copy.start()

    @pl.when(grid == last)
    def _():
        upper[:half] = jnp.zeros_like(upper[:half])
        share[0, 2] = jnp.zeros_like(share[0, 2])
        share[1, 2] = jnp.zeros_like(share[1, 2])
        share[2, 1] = jnp.zeros_like(share[2, 1])

    @pl.when(grid >= last - 1)
    def _():
        share[2, 2] = jnp.zeros_like(share[2, 2])

    @pl.when(grid == 0)
    def _():
        share[0, 0] = jnp.zeros_like(share[0, 0])
        share[1, 0] = jnp.zeros_like(share[1, 0])
        share[2, 0] = jnp.zeros_like(share[2, 0])

    ones = jnp.ones((height, width), jnp.float32)
    totals = []
    for layer in (0, 1, -1):
        place = grid * depth + layer

        def inside(steps):
            low = jnp.minimum(jnp.maximum(place - steps + 1, 0), 1)
            high = jnp.minimum(jnp.maximum(layers * depth - place - steps, 0), 1)
            return (low + high).astype(jnp.float32) * ones

        totals.append(along_rows(ring_columns(ones, inside(1), inside(2))))

    sides = jnp.minimum(grid, 2) + jnp.minimum(last - grid, 2)
    pl.semaphore_wait(barrier, groups - 1 + groups * sides)

    def plane_copy(index):
        up = index >= half
        return pltpu.make_async_remote_copy(
            src_ref=modes_ref.at[index, :, depth - 1 if up else 0],
            dst_ref=upper.at[index],
            send_sem=plane_send.at[index],
            recv_sem=plane_recv.at[index],
            device_id=target(1 if up else -1, 0),
            device_id_type=MESH,
        )

    def density_up():
        return pltpu.make_async_remote_copy(
            src_ref=density_ref.at[depth - 1],
            dst_ref=dens.at[depth],
            send_sem=plane_send.at[count],
            recv_sem=plane_recv.at[count],
            device_id=target(1, 0),
            device_id_type=MESH,
        )

    def arriving(index):
        return pltpu.make_async_remote_copy(
            src_ref=modes_ref.at[index, :, 0],
            dst_ref=upper.at[index],
            send_sem=plane_send.at[index],
            recv_sem=plane_recv.at[index],
            device_id=target(0, 0),
            device_id_type=MESH,
        )

    down, up = range(half), range(half, count)
    for one, two in zip(down, up):
        there(-1, lambda: plane_copy(one).start())
        there(1, lambda: plane_copy(two).start())
    there(1, lambda: density_up().start())

    zeros = jnp.zeros((height, width), jnp.float32)

    def first(index, carry):
        low = [plane_terms(field[index, component, 0]) for component in range(3)]
        high = [plane_terms(field[index, component, 1]) for component in range(3)]
        kept = jnp.where(index < half, 1.0, 0.0)
        for component in range(3):
            for pattern in range(4):
                top, bottom = high[component][pattern], low[component][pattern]
                terms[index, component, pattern] = kept * top + (1.0 - kept) * bottom
        stiff, mass = element_form(low, high)
        return carry[0] + stiff, carry[1] + eigen_ref[index] * mass

    def kept_terms(index):
        return [[terms[index, component, pattern] for pattern in range(4)] for component in range(3)]

    def add_form(layer, index, low, high):
        stiff, mass = element_form(low, high)
        sums[layer, 0] += stiff
        sums[layer, 1] += eigen_ref[index] * mass

    reach = {0: (-1, 1, 0), 1: (-1, 1, 0), 2: (-2, -1, 0)}

    def sends(kind):
        return [(step, turn) for step in reach[kind] for turn in range(groups) if (step, turn) != (0, 0)]

    def slot(kind, source):
        return source if kind == 2 else source + 1

    def share_copy(kind, step, turn):
        return pltpu.make_async_remote_copy(
            src_ref=share.at[kind, slot(kind, 0), mode],
            dst_ref=share.at[kind, slot(kind, -step), mode],
            send_sem=share_send.at[kind, slot(kind, -step), turn],
            recv_sem=share_recv.at[kind, slot(kind, -step), mode],
            device_id=target(step, turn),
            device_id_type=MESH,
        )

    def arrived(kind, source, turn):
        group = lax.rem(mode + turn, groups)
        return pltpu.make_async_remote_copy(
            src_ref=share.at[kind, slot(kind, 0), mode],
            dst_ref=share.at[kind, slot(kind, source), group],
            send_sem=share_send.at[kind, slot(kind, source), turn],
            recv_sem=share_recv.at[kind, slot(kind, source), group],
            device_id=target(0, 0),
            device_id_type=MESH,
        )

    def finish(kind, density, stiff, mass):
        slope = 3.0 * (1.0 - 0.001) * density * density
        share[kind, slot(kind, 0), mode] = ((slope * stiff - mass) / totals[kind]).astype(jnp.bfloat16)
        for step, turn in sends(kind):
            there(step, lambda: share_copy(kind, step, turn).start())

    eigen_copy.wait()
    for index in range(count):
        load(index).wait()
    stiff, mass = lax.fori_loop(0, count, first, (zeros, zeros), unroll=2)
    density_copy.wait()
    finish(0, dens[0], stiff, mass)
    sums[...] = jnp.zeros_like(sums)

    @pl.when(grid == last)
    def _():
        @pl.loop(half, count)
        def _(index):
            low = [plane_terms(field[index, component, 1]) for component in range(3)]
            add_form(0, index, low, [[zeros] * 4] * 3)

    @pl.loop(0, half)
    def _(index):
        @pl.when(grid < last)
        def _():
            arriving(index).wait_recv()

        add_form(0, index, kept_terms(index), [plane_terms(upper[index, component]) for component in range(3)])

    finish(1, dens[1], sums[0, 0], sums[0, 1])

    @pl.when(grid > 0)
    def _():
        @pl.loop(half, count)
        def _(index):
            arriving(index).wait_recv()
            add_form(1, index, [plane_terms(upper[index, component]) for component in range(3)], kept_terms(index))

        density_up().wait_recv()
        finish(2, dens[depth], sums[1, 0], sums[1, 1])

    def whole(kind, place):
        return add_all(share[kind, place, group].astype(jnp.float32) for group in range(groups))

    def await_kind(kind):
        for step, turn in reversed(sends(kind)):
            pair = functools.partial(there, -step)
            body = lambda: arrived(kind, -step, turn).wait_recv()
            if kind == 2 and step == 0:
                pl.when(grid > 0)(body)
            else:
                pair(body)
        return [whole(kind, place) for place in range(3)]

    below, centre, above = await_kind(0)
    early = [ring_columns(centre, None, below + above), ring_columns(None, centre + above, None)]
    below, centre, above = [one + two for one, two in zip(await_kind(1), await_kind(2))]
    late = [ring_columns(None, below + centre, None), ring_columns(centre, None, below + above)]
    for layer in range(depth):
        out_ref[layer] = along_rows([one + two for one, two in zip(early[layer], late[layer])])

    for kind in range(3):
        for step, turn in sends(kind):
            body = lambda: share_copy(kind, step, turn).wait_send()
            if kind == 2 and step == 0:
                pl.when(grid > 0)(body)
            else:
                there(step, body)
    for one, two in zip(down, up):
        there(-1, lambda: plane_copy(one).wait_send())
        there(1, lambda: plane_copy(two).wait_send())
    there(1, lambda: density_up().wait_send())


def local(layers, groups, modes, eigenvalues, density):
    count, _, depth, height, width = modes.shape
    assert depth == 2 and count % 2 == 0
    return pl.pallas_call(
        functools.partial(kernel, layers, groups),
        out_shape=pltpu.VMEM(density.shape, jnp.float32),
        in_specs=[
            pl.BlockSpec(memory_space=pltpu.HBM),
            pl.BlockSpec(memory_space=pltpu.HBM),
            pl.BlockSpec(memory_space=pltpu.HBM),
        ],
        out_specs=pl.BlockSpec(memory_space=pltpu.VMEM),
        scratch_shapes=[
            pltpu.SMEM(eigenvalues.shape, jnp.float32),
            pltpu.VMEM(modes.shape, jnp.bfloat16),
            pltpu.VMEM((count, 3, height, width), jnp.bfloat16),
            pltpu.VMEM((count, 3, 4, height, width), jnp.float32),
            pltpu.VMEM((depth + 1, height, width), jnp.float32),
            pltpu.VMEM((3, 3, groups, height, width), jnp.bfloat16),
            pltpu.VMEM((2, 2, height, width), jnp.float32),
            pltpu.SemaphoreType.DMA,
            pltpu.SemaphoreType.DMA((count,)),
            pltpu.SemaphoreType.DMA,
            pltpu.SemaphoreType.DMA((count + 1,)),
            pltpu.SemaphoreType.DMA((count + 1,)),
            pltpu.SemaphoreType.DMA((3, 3, groups)),
            pltpu.SemaphoreType.DMA((3, 3, groups)),
        ],
        compiler_params=pltpu.CompilerParams(
            collective_id=0, has_side_effects=True, vmem_limit_bytes=60 * 1024 * 1024
        ),
        name="sensitivities",
    )(modes, eigenvalues, density)


def solution(mesh):
    in_specs = (P("mode", None, "grid", None, None), P("mode"), P("grid", None, None))
    body = functools.partial(local, mesh.shape["grid"], mesh.shape["mode"])
    return jax.shard_map(body, mesh=mesh, in_specs=in_specs, out_specs=P("grid", None, None), check_vma=False)
```

```python
import functools

import jax
import jax.numpy as jnp
import ml_dtypes
import numpy as np
from jax import lax
from jax.experimental import pallas as pl
from jax.experimental.pallas import tpu as pltpu
from jax.sharding import PartitionSpec as P

MESH = pl.DeviceIdType.MESH


def element_tables():
    poisson = 0.3
    lame_first = poisson / ((1.0 + poisson) * (1.0 - 2.0 * poisson))
    shear = 0.5 / (1.0 + poisson)
    elastic = np.zeros((6, 6))
    elastic[:3, :3] = lame_first
    for axis_bit in range(3):
        elastic[axis_bit, axis_bit] += 2.0 * shear
        elastic[axis_bit + 3, axis_bit + 3] = shear
    stiffness = np.zeros((24, 24))
    mass_small = np.zeros((8, 8))
    point = 1.0 / np.sqrt(3.0)
    for gauss in range(8):
        coords = [point * (2 * (gauss >> axis_bit & 1) - 1) for axis_bit in range(3)]
        shape_values = np.zeros(8)
        grads = np.zeros((3, 8))
        for corner in range(8):
            signs = [2 * (corner >> axis_bit & 1) - 1 for axis_bit in range(3)]
            factors = [1.0 + signs[axis_bit] * coords[axis_bit] for axis_bit in range(3)]
            shape_values[corner] = 0.125 * factors[0] * factors[1] * factors[2]
            grads[0, corner] = 0.25 * signs[0] * factors[1] * factors[2]
            grads[1, corner] = 0.25 * signs[1] * factors[0] * factors[2]
            grads[2, corner] = 0.25 * signs[2] * factors[0] * factors[1]
        strain = np.zeros((6, 24))
        for corner in range(8):
            column = 3 * corner
            strain[0, column] = grads[0, corner]
            strain[1, column + 1] = grads[1, corner]
            strain[2, column + 2] = grads[2, corner]
            strain[3, column] = grads[1, corner]
            strain[3, column + 1] = grads[0, corner]
            strain[4, column + 1] = grads[2, corner]
            strain[4, column + 2] = grads[1, corner]
            strain[5, column] = grads[2, corner]
            strain[5, column + 2] = grads[0, corner]
        stiffness = stiffness + strain.T @ elastic @ strain * 0.125
        mass_small = mass_small + np.outer(shape_values, shape_values) * 0.125
    mass = np.kron(mass_small, np.eye(3))
    return np.concatenate([stiffness, mass], 0).astype(np.float32)


def transformed_terms():
    table = element_tables().astype(ml_dtypes.bfloat16).astype(np.float64)
    change = np.ones((8, 8))
    for corner in range(8):
        for pattern in range(8):
            for bit in range(3):
                if pattern >> bit & 1 and not corner >> bit & 1:
                    change[corner, pattern] *= -1.0
    stiff, mass = (
        np.einsum("is,icjd,jt->sctd", change, part.reshape(8, 3, 8, 3), change).reshape(24, 24) / 64.0
        for part in (table[:24], table[24:])
    )
    assert np.abs(mass - np.diag(np.diag(mass))).max() < 1e-12
    squares, crosses = {}, {}
    for row in range(24):
        key = (round(stiff[row, row], 12), round(mass[row, row], 12))
        squares.setdefault(key, []).append(row)
        for column in range(row):
            value = round(stiff[row, column] + stiff[column, row], 12)
            if value != 0.0:
                crosses.setdefault(value, []).append((row, column))
    return squares, crosses


def next_in(value, axis):
    size = value.shape[axis]
    place = lax.broadcasted_iota(jnp.int32, value.shape, axis)
    return jnp.where(place == size - 1, 0.0, pltpu.roll(value, size - 1, axis))


def both_sides(value, steps, axis):
    size = value.shape[axis]
    place = lax.broadcasted_iota(jnp.int32, value.shape, axis)
    ahead = jnp.where(place >= size - steps, 0.0, pltpu.roll(value, size - steps, axis))
    behind = jnp.where(place < steps, 0.0, pltpu.roll(value, steps, axis))
    return ahead + behind


def plane_terms(plane):
    value = plane.astype(jnp.float32)
    ahead = next_in(value, 1)
    along_x = (value + ahead, ahead - value)
    shifted = [next_in(part, 0) for part in along_x]
    return [along_x[0] + shifted[0], along_x[1] + shifted[1], shifted[0] - along_x[0], shifted[1] - along_x[1]]


def add_all(values):
    values = list(values)
    while len(values) > 1:
        values = [sum(values[i : i + 2][1:], values[i]) for i in range(0, len(values), 2)]
    return values[0]


def element_form(low, high):
    squares, crosses = transformed_terms()
    wave = {}
    for component in range(3):
        for pattern in range(4):
            wave[3 * pattern + component] = low[component][pattern] + high[component][pattern]
            wave[3 * (pattern + 4) + component] = high[component][pattern] - low[component][pattern]
    stiff, by_mass = [], {}
    for (stiff_value, mass_value), rows in squares.items():
        total = add_all(wave[row] * wave[row] for row in rows)
        if stiff_value != 0.0:
            stiff.append(stiff_value * total)
        by_mass.setdefault(mass_value, []).append(total)
    for value, pairs in crosses.items():
        stiff.append(value * add_all(wave[row] * wave[column] for row, column in pairs))
    mass = [value * add_all(totals) for value, totals in by_mass.items()]
    return add_all(stiff), add_all(mass)


def ring_columns(near, one, two):
    def weight(square):
        return max(0.0, 2.5 - float(np.sqrt(square)))

    rings = []
    for square, layer in ((0, near), (1, one), (4, two)):
        if layer is not None:
            rings.append((square, layer))
            for steps in (1, 2):
                if weight(square + steps * steps) > 0.0:
                    rings.append((square + steps * steps, both_sides(layer, steps, 0)))
    gathered = {}
    for square, ring in rings:
        gathered.setdefault(square, []).append(ring)
    gathered = {square: add_all(parts) for square, parts in gathered.items()}
    return [
        add_all(
            weight(square + steps * steps) * ring
            for square, ring in gathered.items()
            if weight(square + steps * steps) > 0.0
        )
        for steps in range(3)
    ]


def along_rows(columns):
    return columns[0] + both_sides(columns[1], 1, 1) + both_sides(columns[2], 2, 1)


def kernel(
    layers, groups, modes_ref, eigenvalues_ref, density_ref, out_ref,
    eigen_ref, field, upper, terms, dens, share, sums,
    eigen_sem, field_sem, dens_sem, plane_send, plane_recv, share_send, share_recv,
):
    grid, mode = lax.axis_index("grid"), lax.axis_index("mode")
    count, depth = modes_ref.shape[0], modes_ref.shape[2]
    height, width = modes_ref.shape[3:]
    last = layers - 1

    partners = [(step, turn) for step in (-2, 2, -1, 1, 0) for turn in range(groups) if (step, turn) != (0, 0)]
    half = count // 2

    def target(step, turn):
        return (grid + step, lax.rem(mode + turn, groups))

    def there(step, body):
        if step < 0:
            pl.when(grid + step >= 0)(body)
        elif step > 0:
            pl.when(grid + step <= last)(body)
        else:
            body()

    barrier = pltpu.get_barrier_semaphore()
    for step, turn in partners:
        there(step, lambda: pl.semaphore_signal(barrier, inc=1, device_id=target(step, turn), device_id_type=MESH))

    def load(index):
        return pltpu.make_async_copy(modes_ref.at[index], field.at[index], field_sem.at[index])

    eigen_copy = pltpu.make_async_copy(eigenvalues_ref, eigen_ref, eigen_sem)
    eigen_copy.start()
    for index in range(count):
        load(index).start()
    density_copy = pltpu.make_async_copy(density_ref, dens.at[:depth], dens_sem)
    density_copy.start()

    @pl.when(grid == last)
    def _():
        upper[:half] = jnp.zeros_like(upper[:half])
        share[0, 2] = jnp.zeros_like(share[0, 2])
        share[1, 2] = jnp.zeros_like(share[1, 2])
        share[2, 1] = jnp.zeros_like(share[2, 1])

    @pl.when(grid >= last - 1)
    def _():
        share[2, 2] = jnp.zeros_like(share[2, 2])

    @pl.when(grid == 0)
    def _():
        share[0, 0] = jnp.zeros_like(share[0, 0])
        share[1, 0] = jnp.zeros_like(share[1, 0])
        share[2, 0] = jnp.zeros_like(share[2, 0])

    ones = jnp.ones((height, width), jnp.float32)
    totals = []
    for layer in (0, 1, -1):
        place = grid * depth + layer

        def inside(steps):
            low = jnp.minimum(jnp.maximum(place - steps + 1, 0), 1)
            high = jnp.minimum(jnp.maximum(layers * depth - place - steps, 0), 1)
            return (low + high).astype(jnp.float32) * ones

        totals.append(along_rows(ring_columns(ones, inside(1), inside(2))))

    sides = jnp.minimum(grid, 2) + jnp.minimum(last - grid, 2)
    pl.semaphore_wait(barrier, groups - 1 + groups * sides)

    def plane_copy(index):
        up = index >= half
        return pltpu.make_async_remote_copy(
            src_ref=modes_ref.at[index, :, depth - 1 if up else 0],
            dst_ref=upper.at[index],
            send_sem=plane_send.at[index],
            recv_sem=plane_recv.at[index],
            device_id=target(1 if up else -1, 0),
            device_id_type=MESH,
        )

    def density_up():
        return pltpu.make_async_remote_copy(
            src_ref=density_ref.at[depth - 1],
            dst_ref=dens.at[depth],
            send_sem=plane_send.at[count],
            recv_sem=plane_recv.at[count],
            device_id=target(1, 0),
            device_id_type=MESH,
        )

    def arriving(index):
        return pltpu.make_async_remote_copy(
            src_ref=modes_ref.at[index, :, 0],
            dst_ref=upper.at[index],
            send_sem=plane_send.at[index],
            recv_sem=plane_recv.at[index],
            device_id=target(0, 0),
            device_id_type=MESH,
        )

    down, up = range(half), range(half, count)
    for one, two in zip(down, up):
        there(-1, lambda: plane_copy(one).start())
        there(1, lambda: plane_copy(two).start())
    there(1, lambda: density_up().start())

    zeros = jnp.zeros((height, width), jnp.float32)

    def first(index, carry):
        low = [plane_terms(field[index, component, 0]) for component in range(3)]
        high = [plane_terms(field[index, component, 1]) for component in range(3)]
        kept = jnp.where(index < half, 1.0, 0.0)
        for component in range(3):
            for pattern in range(4):
                top, bottom = high[component][pattern], low[component][pattern]
                terms[index, component, pattern] = kept * top + (1.0 - kept) * bottom
        stiff, mass = element_form(low, high)
        return carry[0] + stiff, carry[1] + eigen_ref[index] * mass

    def kept_terms(index):
        return [[terms[index, component, pattern] for pattern in range(4)] for component in range(3)]

    def add_form(layer, index, low, high):
        stiff, mass = element_form(low, high)
        sums[layer, 0] += stiff
        sums[layer, 1] += eigen_ref[index] * mass

    reach = {0: (-1, 1, 0), 1: (-1, 1, 0), 2: (-2, -1, 0)}

    def sends(kind):
        return [(step, turn) for step in reach[kind] for turn in range(groups) if (step, turn) != (0, 0)]

    def slot(kind, source):
        return source if kind == 2 else source + 1

    def share_copy(kind, step, turn):
        return pltpu.make_async_remote_copy(
            src_ref=share.at[kind, slot(kind, 0), mode],
            dst_ref=share.at[kind, slot(kind, -step), mode],
            send_sem=share_send.at[kind, slot(kind, -step), turn],
            recv_sem=share_recv.at[kind, slot(kind, -step), mode],
            device_id=target(step, turn),
            device_id_type=MESH,
        )

    def arrived(kind, source, turn):
        group = lax.rem(mode + turn, groups)
        return pltpu.make_async_remote_copy(
            src_ref=share.at[kind, slot(kind, 0), mode],
            dst_ref=share.at[kind, slot(kind, source), group],
            send_sem=share_send.at[kind, slot(kind, source), turn],
            recv_sem=share_recv.at[kind, slot(kind, source), group],
            device_id=target(0, 0),
            device_id_type=MESH,
        )

    def finish(kind, density, stiff, mass):
        slope = 3.0 * (1.0 - 0.001) * density * density
        share[kind, slot(kind, 0), mode] = ((slope * stiff - mass) / totals[kind]).astype(jnp.bfloat16)
        for step, turn in sends(kind):
            there(step, lambda: share_copy(kind, step, turn).start())

    eigen_copy.wait()
    for index in range(count):
        load(index).wait()
    stiff, mass = lax.fori_loop(0, count, first, (zeros, zeros), unroll=2)
    density_copy.wait()
    finish(0, dens[0], stiff, mass)
    sums[...] = jnp.zeros_like(sums)

    @pl.when(grid > 0)
    def _():
        @pl.loop(half, count)
        def _(index):
            arriving(index).wait_recv()
            add_form(1, index, [plane_terms(upper[index, component]) for component in range(3)], kept_terms(index))

        density_up().wait_recv()
        finish(2, dens[depth], sums[1, 0], sums[1, 1])

    @pl.when(grid == last)
    def _():
        @pl.loop(half, count)
        def _(index):
            low = [plane_terms(field[index, component, 1]) for component in range(3)]
            add_form(0, index, low, [[zeros] * 4] * 3)

    @pl.loop(0, half)
    def _(index):
        @pl.when(grid < last)
        def _():
            arriving(index).wait_recv()

        add_form(0, index, kept_terms(index), [plane_terms(upper[index, component]) for component in range(3)])

    finish(1, dens[1], sums[0, 0], sums[0, 1])

    def whole(kind, place):
        return add_all(share[kind, place, group].astype(jnp.float32) for group in range(groups))

    def await_kind(kind):
        for step, turn in reversed(sends(kind)):
            pair = functools.partial(there, -step)
            body = lambda: arrived(kind, -step, turn).wait_recv()
            if kind == 2 and step == 0:
                pl.when(grid > 0)(body)
            else:
                pair(body)
        return [whole(kind, place) for place in range(3)]

    below, centre, above = await_kind(0)
    early = [ring_columns(centre, None, below + above), ring_columns(None, centre + above, None)]
    below, centre, above = [one + two for one, two in zip(await_kind(1), await_kind(2))]
    late = [ring_columns(None, below + centre, None), ring_columns(centre, None, below + above)]
    for layer in range(depth):
        out_ref[layer] = along_rows([one + two for one, two in zip(early[layer], late[layer])])

    for kind in range(3):
        for step, turn in sends(kind):
            body = lambda: share_copy(kind, step, turn).wait_send()
            if kind == 2 and step == 0:
                pl.when(grid > 0)(body)
            else:
                there(step, body)
    for one, two in zip(down, up):
        there(-1, lambda: plane_copy(one).wait_send())
        there(1, lambda: plane_copy(two).wait_send())
    there(1, lambda: density_up().wait_send())


def local(layers, groups, modes, eigenvalues, density):
    count, _, depth, height, width = modes.shape
    assert depth == 2 and count % 2 == 0
    return pl.pallas_call(
        functools.partial(kernel, layers, groups),
        out_shape=pltpu.VMEM(density.shape, jnp.float32),
        in_specs=[
            pl.BlockSpec(memory_space=pltpu.HBM),
            pl.BlockSpec(memory_space=pltpu.HBM),
            pl.BlockSpec(memory_space=pltpu.HBM),
        ],
        out_specs=pl.BlockSpec(memory_space=pltpu.VMEM),
        scratch_shapes=[
            pltpu.SMEM(eigenvalues.shape, jnp.float32),
            pltpu.VMEM(modes.shape, jnp.bfloat16),
            pltpu.VMEM((count, 3, height, width), jnp.bfloat16),
            pltpu.VMEM((count, 3, 4, height, width), jnp.float32),
            pltpu.VMEM((depth + 1, height, width), jnp.float32),
            pltpu.VMEM((3, 3, groups, height, width), jnp.bfloat16),
            pltpu.VMEM((2, 2, height, width), jnp.float32),
            pltpu.SemaphoreType.DMA,
            pltpu.SemaphoreType.DMA((count,)),
            pltpu.SemaphoreType.DMA,
            pltpu.SemaphoreType.DMA((count + 1,)),
            pltpu.SemaphoreType.DMA((count + 1,)),
            pltpu.SemaphoreType.DMA((3, 3, groups)),
            pltpu.SemaphoreType.DMA((3, 3, groups)),
        ],
        compiler_params=pltpu.CompilerParams(
            collective_id=0, has_side_effects=True, vmem_limit_bytes=60 * 1024 * 1024
        ),
        name="sensitivities",
    )(modes, eigenvalues, density)


def solution(mesh):
    in_specs = (P("mode", None, "grid", None, None), P("mode"), P("grid", None, None))
    body = functools.partial(local, mesh.shape["grid"], mesh.shape["mode"])
    return jax.shard_map(body, mesh=mesh, in_specs=in_specs, out_specs=P("grid", None, None), check_vma=False)
```
